128 devices in a mesh: dp: 16 (over y_lo, x, core), ctx: 8 (over y_hi, z).
Axes of the slice: x: 4, y: 4 (y_hi: 2, y_lo: 2; y = y_hi * 2 + y_lo), z: 4, core: 2. Of those that a mesh axis runs over, the one named last changes fastest.
Arguments:
- tokens: bfloat16 [16, 3072, 4096], P('dp', 'ctx'), may hold values from -64 to 64
- positions: int32 [16, 3072], P('dp', 'ctx'), may hold values from 0 to 3071, each once within a row
- segment_ids: int32 [16, 3072], P('dp'), may hold values from 0 to 7, never falling along the last dimension, each value on 1 to 1536 neighbouring positions
- w_query: bfloat16 [4096, 2048], P('dp'), may hold values from -0.09375 to 0.09375
- key_weight: bfloat16 [4096, 512], P('dp'), may hold values from -0.09375 to 0.09375
- value_weight: bfloat16 [4096, 512], P('dp'), may hold values from -0.09375 to 0.09375
Outputs:
- attended: bfloat16 [16, 3072, 2048], P('dp', 'ctx')
The draws below stay inside these ranges and needn't reach their ends.
Inputs may be any that keep to these rules, and one draw needn't show every extreme that they name: Each row is a permutation of the positions of its sequence. `segment_ids`: never falling along positions; each document 1 to 1536 positions.
All inputs are finite; a program needn't handle non-finite values.
Results may differ from the reference program's by a relative error of at most 0.017.
The reference program's roundings to bfloat16 on the way count: a program that leaves them out, or rounds other values in their place, can miss the bound.
Values may be sent and summed in bfloat16 or wider, within the bound.
A program may use at most 128 MiB of HBM per device.

```python
import math
import jax
import jax.numpy as jnp
import numpy as np
from jax import lax

MODEL_WIDTH = 4096
QUERY_HEADS = 16
KEY_VALUE_HEADS = 4
HEAD_SIZE = 128
DOCS = 8
LEN = 3072
SEQS = 16


def draw_tokens(key, part):
    key = jax.random.fold_in(key, 11)
    base = jax.random.truncated_normal(key, -4.0, 4.0, (SEQS, LEN, MODEL_WIDTH), jnp.float32)
    return base.astype(jnp.bfloat16)


def block_scale(key, dims, pieces, low, top_value):
    level, own = 1.0, jax.random.fold_in(key, 6)
    for axis_at, blocks in pieces:
        steps = jnp.exp(jax.random.uniform(jax.random.fold_in(own, axis_at), (blocks,), jnp.float32, low / len(pieces), top_value / len(pieces)))
        level = level * jnp.repeat(steps, dims[axis_at] // blocks).reshape([-1 if axis == axis_at else 1 for axis in range(len(dims))])
    return level


def length_profile(number_of, total, reach, slope):
    portions = [(1 << 20) // math.isqrt(rank ** slope) + 1 for rank in range(2, number_of + 1)]
    spare, given = total - reach - (number_of - 1), [1] * (number_of - 1)
    while spare > 0:
        candidates = [i for i in range(number_of - 1) if given[i] < reach]
        pool, remaining = sum([portions[i] for i in candidates]), spare
        for i in candidates:
            more = min(reach - given[i], max(1, remaining * portions[i] // pool), spare)
            given[i] = given[i] + more
            spare = spare - more
    return np.array([reach] + given)


def ragged_sizes(rng, count, total, limit, slope):
    if count == 2:
        one = jax.random.randint(rng, (), max(1, total - limit), min(limit, total - 1) + 1)
        return jnp.stack([one, total - one])
    tallies = jnp.asarray(length_profile(count, total, limit, slope), jnp.int32)
    twos = (count - 1) // 2
    giver, sink = tallies[1:1 + 2 * twos:2], tallies[2:2 + 2 * twos:2]
    margin = jnp.minimum(giver - 1, limit - sink)
    moved = jax.random.randint(jax.random.fold_in(rng, 1), (twos,), 0, 1 << 20) % (margin + 1)
    tallies = tallies.at[1:1 + 2 * twos:2].set(giver - moved).at[2:2 + 2 * twos:2].set(sink + moved)
    return tallies[jax.random.permutation(jax.random.fold_in(rng, 2), count)]


def gaussian(rng, dims, spread, most, shards=(), held_as=jnp.bfloat16):
    array = jax.random.normal(rng, dims, jnp.float32) * spread
    if len(shards) > 0:
        array = block_scale(rng, dims, shards, -0.22, 0.18) * array
    return jnp.clip(array, min=-most, max=most).astype(held_as)


def setup_inputs(seed: int = 0) -> dict:
    key_list = jax.random.split(jax.random.key(seed), 7)
    tokens = draw_tokens(jax.random.fold_in(key_list[6], 71), 0)
    positions = jax.vmap(lambda own: jax.random.permutation(own, LEN))(jax.random.split(key_list[1], SEQS)).reshape((SEQS, LEN)).astype(jnp.int32)
    segment_ids = jax.vmap(lambda own: jnp.searchsorted(jnp.cumsum(ragged_sizes(own, DOCS, LEN, LEN // 2, 2)), jnp.arange(LEN), side="right"))(jax.random.split(key_list[2], SEQS)).reshape((SEQS, LEN)).astype(jnp.int32)
    w_query = gaussian(key_list[3], (MODEL_WIDTH, QUERY_HEADS * HEAD_SIZE), MODEL_WIDTH ** -0.5, 0.09375, ((0, 16),))
    key_weight = gaussian(key_list[4], (MODEL_WIDTH, KEY_VALUE_HEADS * HEAD_SIZE), MODEL_WIDTH ** -0.5, 0.09375, ((0, 16),))
    value_weight = gaussian(key_list[5], (MODEL_WIDTH, KEY_VALUE_HEADS * HEAD_SIZE), MODEL_WIDTH ** -0.5, 0.09375, ((0, 16),))
    return {"tokens": tokens, "positions": positions, "segment_ids": segment_ids, "w_query": w_query, "key_weight": key_weight, "value_weight": value_weight}


def apply_rotary(mat, token_position, heads):
    half = HEAD_SIZE // 2
    freq = 500000.0 ** (-jnp.arange(half, dtype=jnp.float32) / half)
    angle = token_position.astype(jnp.float32)[:, None] * freq[None, :]
    cosine = jnp.cos(angle)[:, None, :]
    sine = jnp.sin(angle)[:, None, :]
    split = mat.reshape(mat.shape[0], heads, HEAD_SIZE)
    first = split[..., :half]
    second = split[..., half:]
    turned = jnp.concatenate([first * cosine - second * sine, second * cosine + first * sine], axis=-1)
    return turned.reshape(mat.shape[0], heads * HEAD_SIZE)


def reference(tokens, positions, segment_ids, w_query, key_weight, value_weight):
    query_group = QUERY_HEADS // KEY_VALUE_HEADS

    def one_sequence(packed):
        token_rows, token_position, documents = packed
        query_matrix = apply_rotary(jnp.dot(token_rows, w_query, preferred_element_type=jnp.float32), token_position, QUERY_HEADS).astype(jnp.bfloat16)
        key = apply_rotary(jnp.dot(token_rows, key_weight, preferred_element_type=jnp.float32), token_position, KEY_VALUE_HEADS).astype(jnp.bfloat16)
        value_matrix = jnp.dot(token_rows, value_weight, preferred_element_type=jnp.float32).astype(jnp.bfloat16)
        seg = documents[token_position]
        visible = (token_position[None, :] <= token_position[:, None]) & (seg[None, :] == seg[:, None])

        def one_head(head):
            kv_head = head // query_group
            q_head = lax.dynamic_slice_in_dim(query_matrix, head * HEAD_SIZE, HEAD_SIZE, 1)
            k_head = lax.dynamic_slice_in_dim(key, kv_head * HEAD_SIZE, HEAD_SIZE, 1)
            v_head = lax.dynamic_slice_in_dim(value_matrix, kv_head * HEAD_SIZE, HEAD_SIZE, 1)
            score = jnp.dot(q_head, k_head.T, preferred_element_type=jnp.float32) * (HEAD_SIZE ** -0.5)
            score = jnp.where(visible, score, -1e30)
            top = jnp.max(score, axis=1, keepdims=True)
            expo = jnp.where(visible, jnp.exp(score - top), 0.0)
            total = jnp.sum(expo, axis=1, keepdims=True)
            summed = jnp.dot(expo.astype(jnp.bfloat16), v_head, preferred_element_type=jnp.float32)
            return summed / total

        outs = lax.map(one_head, jnp.arange(QUERY_HEADS, dtype=jnp.int32))
        return outs.transpose(1, 0, 2).reshape(token_rows.shape[0], QUERY_HEADS * HEAD_SIZE).astype(jnp.bfloat16)

    return lax.map(one_sequence, (tokens, positions, segment_ids))
```

```python
import math

import jax
import jax.numpy as jnp
from jax import lax
from jax.experimental import pallas as pl
from jax.experimental.pallas import tpu as pltpu
from jax.sharding import PartitionSpec as P

QUERY_HEADS = 16
KEY_VALUE_HEADS = 4
HEAD_SIZE = 128
DOCS = 8


def apply_rotary(mat, token_position, heads):
    half = HEAD_SIZE // 2
    freq = 500000.0 ** (-jnp.arange(half, dtype=jnp.float32) / half)
    angle = token_position.astype(jnp.float32)[:, None] * freq[None, :]
    cosine = jnp.cos(angle)[:, None, :]
    sine = jnp.sin(angle)[:, None, :]
    split = mat.reshape(mat.shape[0], heads, HEAD_SIZE)
    first = split[..., :half]
    second = split[..., half:]
    turned = jnp.concatenate(
        [first * cosine - second * sine, second * cosine + first * sine], axis=-1
    )
    return turned.reshape(mat.shape[0], heads * HEAD_SIZE)


RUNS = 8
TOKENS = 384
KEY_BLOCK = 256
QUERY_TILE = 64
GROUP = 4
NEVER = -1e30


def attention_kernel(q_ref, kv_ref, runs_ref, mine_ref, stored_ref, seg_ref, out_ref, key_pos, top, total, summed, rows_done):
    part = KEY_BLOCK // RUNS
    blocks = TOKENS // part
    tiles = TOKENS // QUERY_TILE
    width = GROUP * QUERY_TILE
    factor = HEAD_SIZE ** -0.5 * math.log2(math.e)

    query_pos = mine_ref[...]
    seg = seg_ref[...]
    start = jnp.zeros_like(query_pos)
    for doc in range(1, DOCS):
        before = jnp.sum((seg < doc).astype(jnp.float32), axis=(0, 1), keepdims=True)
        start = jnp.where(before <= query_pos, jnp.maximum(start, before), start)

    runs = runs_ref[...]
    columns = runs.T
    for run in range(RUNS):
        wide = jnp.broadcast_to(columns[:, run : run + 1], (TOKENS, 128))
        key_pos[:, run] = wide.reshape(blocks, part, 128)

    lane = lax.broadcasted_iota(jnp.int32, (1, TOKENS), 1) % part
    lowest = jnp.where(lane == 0, jnp.min(runs, axis=0, keepdims=True), 1e9)
    highest = jnp.where(lane == part - 1, jnp.max(runs, axis=0, keepdims=True), 1e9)

    for tile in range(tiles):
        at = slice(tile * QUERY_TILE, (tile + 1) * QUERY_TILE)
        pos_row = jnp.concatenate([query_pos[:, at]] * GROUP, axis=1)
        start_row = jnp.concatenate([start[:, at]] * GROUP, axis=1)
        last = jnp.max(query_pos[:, at], axis=1, keepdims=True)
        first = jnp.min(start[:, at], axis=1, keepdims=True)
        begin = jnp.sum((highest < first).astype(jnp.int32))
        end = jnp.sum((lowest <= last).astype(jnp.int32))
        top[...] = jnp.full_like(top, NEVER)
        total[...] = jnp.zeros_like(total)
        summed[...] = jnp.zeros_like(summed)
        queries = [
            jnp.concatenate(
                [q_ref[at, (head * GROUP + g) * HEAD_SIZE : (head * GROUP + g + 1) * HEAD_SIZE] for g in range(GROUP)],
                axis=0,
            )
            for head in range(KEY_VALUE_HEADS)
        ]

        def one_block(block, carry):
            rows = pl.ds(pl.multiple_of(block * KEY_BLOCK, KEY_BLOCK), KEY_BLOCK)
            pos = key_pos[block].reshape(KEY_BLOCK, 128)
            pos = jnp.concatenate([pos] * (width // 128), axis=1)
            visible = (pos <= pos_row) & (pos >= start_row)
            for head in range(KEY_VALUE_HEADS):
                at_head = 2 * head * HEAD_SIZE
                keys = kv_ref[rows, at_head : at_head + HEAD_SIZE]
                values = kv_ref[rows, at_head + HEAD_SIZE : at_head + 2 * HEAD_SIZE]
                score = lax.dot_general(
                    keys, queries[head], (((1,), (1,)), ((), ())), preferred_element_type=jnp.float32
                )
                score = jnp.where(visible, score, -jnp.inf)
                old = top[head]
                new = jnp.maximum(old, jnp.max(score, axis=0, keepdims=True))
                weight = jnp.exp2((score - new) * factor)
                fade = jnp.exp2((old - new) * factor)
                top[head] = new
                total[head] = total[head] * fade + jnp.sum(weight, axis=0, keepdims=True)
                added = lax.dot_general(
                    values, weight.astype(jnp.bfloat16), (((0,), (0,)), ((), ())), preferred_element_type=jnp.float32
                )
                summed[head] = summed[head] * fade + added
            return carry

        lax.fori_loop(begin, end, one_block, 0)
        for head in range(KEY_VALUE_HEADS):
            result = (summed[head] / total[head]).astype(jnp.bfloat16)
            for g in range(GROUP):
                rows_done[head * GROUP + g, :, at] = result[:, g * QUERY_TILE : (g + 1) * QUERY_TILE]

    turn = (stored_ref[...] == query_pos).astype(jnp.bfloat16)
    for head in range(QUERY_HEADS):
        out_ref[:, head * HEAD_SIZE : (head + 1) * HEAD_SIZE] = lax.dot_general(
            turn, rows_done[head], (((1,), (1,)), ((), ())), preferred_element_type=jnp.float32
        ).astype(jnp.bfloat16)


def attention(query, kv, runs, mine, stored, seg):
    part = KEY_BLOCK // RUNS
    width = GROUP * QUERY_TILE
    return pl.pallas_call(
        attention_kernel,
        out_shape=jax.ShapeDtypeStruct((TOKENS, QUERY_HEADS * HEAD_SIZE), jnp.bfloat16),
        in_specs=[pl.BlockSpec(memory_space=pltpu.VMEM)] * 6,
        out_specs=pl.BlockSpec(memory_space=pltpu.VMEM),
        scratch_shapes=[
            pltpu.VMEM((TOKENS // part, RUNS, part, 128), jnp.float32),
            pltpu.VMEM((KEY_VALUE_HEADS, 1, width), jnp.float32),
            pltpu.VMEM((KEY_VALUE_HEADS, 1, width), jnp.float32),
            pltpu.VMEM((KEY_VALUE_HEADS, HEAD_SIZE, width), jnp.float32),
            pltpu.VMEM((QUERY_HEADS, HEAD_SIZE, TOKENS), jnp.bfloat16),
        ],
        compiler_params=pltpu.CompilerParams(vmem_limit_bytes=56 << 20),
        cost_estimate=pl.CostEstimate(flops=5 * 10**9, bytes_accessed=11 * 10**6, transcendentals=10**7),
        name="attention",
    )(query, kv, runs, mine, stored, seg)


def shards(tokens, positions, segment_ids, w_query, key_weight, value_weight):
    token_rows, width = tokens.shape[1:]
    flat = tokens.reshape(token_rows, width)
    pos = positions.reshape(-1)
    rank = jnp.sum(pos[None, :] < pos[:, None], axis=1)
    order = (rank[None, :] == jnp.arange(token_rows)[:, None])
    mine = jnp.sum(jnp.where(order, pos[None, :], 0), axis=1)
    flat = jnp.dot(order.astype(jnp.bfloat16), flat, preferred_element_type=jnp.float32).astype(jnp.bfloat16)
    query = jnp.dot(flat, lax.all_gather(w_query, "dp", axis=0, tiled=True), preferred_element_type=jnp.float32)
    both = jnp.concatenate([key_weight, value_weight], axis=1)
    both = jnp.dot(flat, lax.all_gather(both, "dp", axis=0, tiled=True), preferred_element_type=jnp.float32)
    split = KEY_VALUE_HEADS * HEAD_SIZE
    query = apply_rotary(query, mine, QUERY_HEADS).astype(jnp.bfloat16)
    key = apply_rotary(both[:, :split], mine, KEY_VALUE_HEADS).astype(jnp.bfloat16)
    value = both[:, split:].astype(jnp.bfloat16)
    kv = jnp.stack([key.reshape(-1, KEY_VALUE_HEADS, HEAD_SIZE), value.reshape(-1, KEY_VALUE_HEADS, HEAD_SIZE)], axis=2)
    kv = lax.all_gather(kv.reshape(token_rows, 2 * split), "ctx", axis=0)
    runs = lax.all_gather(mine, "ctx", axis=0).astype(jnp.float32)
    part = KEY_BLOCK // RUNS
    kv = kv.reshape(RUNS, token_rows // part, part, 2 * split).transpose(1, 0, 2, 3).reshape(RUNS * token_rows, 2 * split)
    out = attention(
        query,
        kv,
        runs,
        mine.astype(jnp.float32)[None, :],
        pos.astype(jnp.float32)[:, None],
        segment_ids.reshape(-1, 128),
    )
    return out[None]


def solution(mesh):
    placed = (P("dp", "ctx", None), P("dp", "ctx"), P("dp", None), P("dp", None), P("dp", None), P("dp", None))
    return jax.shard_map(
        shards, mesh=mesh, in_specs=placed, out_specs=P("dp", "ctx", None), check_vma=False
    )
```

```python
import math

import jax
import jax.numpy as jnp
from jax import lax
from jax.experimental import pallas as pl
from jax.experimental.pallas import tpu as pltpu
from jax.sharding import PartitionSpec as P

QUERY_HEADS = 16
KEY_VALUE_HEADS = 4
HEAD_SIZE = 128
DOCS = 8


RUNS = 8
TOKENS = 384
KEY_BLOCK = 256
QUERY_TILE = 64
GROUP = 4
NEVER = -1e30


def attention_kernel(q_ref, kv_ref, runs_ref, stored_ref, seg_ref, out_ref, key_pos, top, total, summed, rows_done):
    part = KEY_BLOCK // RUNS
    blocks = TOKENS // part
    tiles = TOKENS // QUERY_TILE
    width = GROUP * QUERY_TILE
    factor = HEAD_SIZE ** -0.5 * math.log2(math.e)

    query_pos = runs_ref[lax.axis_index("ctx")][:1]
    seg = seg_ref[...]
    start = jnp.zeros_like(query_pos)
    for doc in range(1, DOCS):
        before = jnp.sum((seg < doc).astype(jnp.float32), axis=1, keepdims=True)
        start = jnp.where(before <= query_pos, jnp.maximum(start, before), start)

    runs = runs_ref[:, 0]
    columns = runs.T
    for run in range(RUNS):
        wide = jnp.broadcast_to(columns[:, run : run + 1], (TOKENS, 128))
        key_pos[:, run] = wide.reshape(blocks, part, 128)

    lane = lax.broadcasted_iota(jnp.int32, (1, TOKENS), 1) % part
    lowest = jnp.where(lane == 0, jnp.min(runs, axis=0, keepdims=True), 1e9)
    highest = jnp.where(lane == part - 1, jnp.max(runs, axis=0, keepdims=True), 1e9)

    for tile in range(tiles):
        at = slice(tile * QUERY_TILE, (tile + 1) * QUERY_TILE)
        pos_row = jnp.concatenate([query_pos[:, at]] * GROUP, axis=1)
        start_row = jnp.concatenate([start[:, at]] * GROUP, axis=1)
        last = jnp.max(query_pos[:, at], axis=1, keepdims=True)
        first = jnp.min(start[:, at], axis=1, keepdims=True)
        begin = jnp.sum((highest < first).astype(jnp.int32))
        end = jnp.sum((lowest <= last).astype(jnp.int32))
        top[...] = jnp.full_like(top, NEVER)
        total[...] = jnp.zeros_like(total)
        summed[...] = jnp.zeros_like(summed)
        queries = [
            jnp.concatenate(
                [q_ref[head * GROUP + g, at] for g in range(GROUP)],
                axis=0,
            )
            for head in range(KEY_VALUE_HEADS)
        ]

        def one_block(block, carry):
            rows = pl.ds(pl.multiple_of(block * KEY_BLOCK, KEY_BLOCK), KEY_BLOCK)
            pos = key_pos[block].reshape(KEY_BLOCK, 128)
            pos = jnp.concatenate([pos] * (width // 128), axis=1)
            visible = (pos <= pos_row) & (pos >= start_row)
            for head in range(KEY_VALUE_HEADS):
                keys = kv_ref[head, rows, :HEAD_SIZE]
                values = kv_ref[head, rows, HEAD_SIZE:]
                score = lax.dot_general(
                    keys, queries[head], (((1,), (1,)), ((), ())), preferred_element_type=jnp.float32
                )
                score = jnp.where(visible, score, -jnp.inf)
                old = top[head]
                new = jnp.maximum(old, jnp.max(score, axis=0, keepdims=True))
                weight = jnp.exp2((score - new) * factor)
                fade = jnp.exp2((old - new) * factor)
                top[head] = new
                total[head] = total[head] * fade + jnp.sum(weight, axis=0, keepdims=True)
                added = lax.dot_general(
                    values, weight.astype(jnp.bfloat16), (((0,), (0,)), ((), ())), preferred_element_type=jnp.float32
                )
                summed[head] = summed[head] * fade + added
            return carry

        lax.fori_loop(begin, end, one_block, 0)
        for head in range(KEY_VALUE_HEADS):
            result = (summed[head] / total[head]).astype(jnp.bfloat16)
            for g in range(GROUP):
                rows_done[head * GROUP + g, :, at] = result[:, g * QUERY_TILE : (g + 1) * QUERY_TILE]

    stored = jnp.broadcast_to(stored_ref[...].astype(jnp.float32), (8, TOKENS)).T[:, :1]
    turn = (stored == query_pos).astype(jnp.bfloat16)
    for head in range(QUERY_HEADS):
        out_ref[:, head * HEAD_SIZE : (head + 1) * HEAD_SIZE] = lax.dot_general(
            turn, rows_done[head], (((1,), (1,)), ((), ())), preferred_element_type=jnp.float32
        ).astype(jnp.bfloat16)


def attention(query, kv, runs, stored, seg):
    part = KEY_BLOCK // RUNS
    width = GROUP * QUERY_TILE
    return pl.pallas_call(
        attention_kernel,
        out_shape=jax.ShapeDtypeStruct((TOKENS, QUERY_HEADS * HEAD_SIZE), jnp.bfloat16),
        in_specs=[pl.BlockSpec(memory_space=pltpu.VMEM)] * 5,
        out_specs=pl.BlockSpec(memory_space=pltpu.VMEM),
        scratch_shapes=[
            pltpu.VMEM((TOKENS // part, RUNS, part, 128), jnp.float32),
            pltpu.VMEM((KEY_VALUE_HEADS, 1, width), jnp.float32),
            pltpu.VMEM((KEY_VALUE_HEADS, 1, width), jnp.float32),
            pltpu.VMEM((KEY_VALUE_HEADS, HEAD_SIZE, width), jnp.float32),
            pltpu.VMEM((QUERY_HEADS, HEAD_SIZE, TOKENS), jnp.bfloat16),
        ],
        compiler_params=pltpu.CompilerParams(vmem_limit_bytes=56 << 20),
        cost_estimate=pl.CostEstimate(flops=5 * 10**9, bytes_accessed=11 * 10**6, transcendentals=10**7),
        name="attention",
    )(query, kv, runs, stored, seg)


ROWS = 256
CHIPS = 8
CHUNK = 2 * ROWS
COPIES = 128
PART = KEY_BLOCK // RUNS
BLOCKS = TOKENS // PART


def projection_kernel(
    tokens, positions, freq, w_query, w_key, w_value,
    q_out, kv_out, pos_out,
    stored, tok, weights_a, weights_b, weights_c, weights_d,
    acc_a, acc_b, acc_c, acc_d, tables, kv_stage, q_stage, pos_stage,
    local_sem, send_sem, recv_sem,
):
    dp, ctx = lax.axis_index("dp"), lax.axis_index("ctx")
    core, x, y_lo = dp % 2, (dp // 2) % 4, dp // 8
    y_hi, z = ctx // 4, ctx % 4
    other = 1 - core

    def device(core=core, x=x, y_lo=y_lo, y_hi=y_hi, z=z):
        return ((y_lo * 4 + x) * 2 + core, y_hi * 4 + z)

    right, left, across = (x + 1) % 4, (x + 3) % 4, (x + 2) % 4
    z_right, z_left = (z + 1) % 4, (z + 3) % 4
    far = 1 - y_lo
    y_up = device(y_lo=far, y_hi=(y_hi + y_lo) % 2)
    y_down = device(y_lo=far, y_hi=(y_hi + far) % 2)
    x_up, x_down = device(x=right), device(x=left)
    z_up, z_down = device(z=z_right), device(z=z_left)
    sibling = device(core=other)
    opposite = device(y_hi=1 - y_hi)

    locals_, copies = [], []

    def local(src, dst):
        copy = pltpu.make_async_copy(src, dst, local_sem.at[len(locals_)])
        locals_.append(copy)
        copy.start()
        return copy

    def remote(src, dst, to):
        at = len(copies)
        copy = pltpu.make_async_remote_copy(
            src_ref=src, dst_ref=dst, send_sem=send_sem.at[at], recv_sem=recv_sem.at[at],
            device_id=to, device_id_type=pl.DeviceIdType.MESH,
        )
        copies.append(copy)
        copy.start()
        return copy

    def chip(x, row=y_lo):
        return row * 4 + x

    def columns(ref, start, size):
        return ref.at[:, pl.ds(pl.multiple_of(start, size), size)]

    me = chip(x)
    half = HEAD_SIZE
    buffers = (weights_a, weights_b, weights_c, weights_d)
    totals = (acc_a, acc_b, acc_c, acc_d)

    def sources(piece, of_core):
        if piece < 2:
            start = (of_core * 2 + piece) * half
            return [(columns(w_key, start, half), slice(0, half)), (columns(w_value, start, half), slice(half, 2 * half))]
        start = (of_core * 2 + piece - 2) * 4 * half
        return [(columns(w_query, start, 4 * half), slice(0, 4 * half))]

    own = [[local(src, buffers[p].at[me, core, :, to]) for src, to in sources(p, core)] for p in (0, 1)]
    read = local(tokens, stored)
    own += [[local(src, buffers[p].at[me, core, :, to]) for src, to in sources(p, core)] for p in (2, 3)]

    barrier = pltpu.get_barrier_semaphore()
    partners = (sibling, x_up, x_down, y_up, y_down, z_up, z_down, opposite)
    for partner in partners:
        pl.semaphore_signal(barrier, inc=1, device_id=partner, device_id_type=pl.DeviceIdType.MESH)
    pl.semaphore_wait(barrier, len(partners))

    def to_sibling(piece):
        return [remote(src, buffers[piece].at[me, core, :, to], sibling) for src, to in sources(piece, other)]

    def unit(piece, at, row, to):
        ref = buffers[piece].at[at, row]
        return remote(ref, ref, to)

    def send_x(piece, at, row):
        return unit(piece, at, row, x_up), unit(piece, at, row, x_down)

    def send_y(piece, at):
        return unit(piece, at, core, y_up), unit(piece, at, other, y_down)

    def arrive(*some):
        for copy in some:
            copy.wait_recv()

    def add(piece, at, first=False):
        weights = buffers[piece][at]
        product = jnp.dot(
            tok[at], weights.reshape(CHUNK, weights.shape[-1]), preferred_element_type=jnp.float32
        )
        if first:
            totals[piece][...] = product
        else:
            totals[piece][...] += product

    sib = [to_sibling(0), to_sibling(1)]
    x1, y1 = {}, {}

    def start_x(piece, row):
        for copy in own[piece]:
            copy.wait()
        x1[piece] = [send_x(piece, row, core)]

    def finish_x(piece, row):
        arrive(*sib[piece])
        x1[piece].append(send_x(piece, row, other))

    for piece in (0, 1):
        start_x(piece, me)
    for piece in (0, 1):
        finish_x(piece, me)
        y1[piece] = {0: send_y(piece, me)}
    sib += [to_sibling(2), to_sibling(3)]

    pos_row = positions[...].astype(jnp.float32)
    pos_col = jnp.broadcast_to(pos_row, (8, TOKENS)).T[:, :1]
    rank_row = jnp.sum((pos_col < pos_row).astype(jnp.float32), axis=0, keepdims=True)
    rank_col = jnp.sum((pos_row < pos_col).astype(jnp.float32), axis=1, keepdims=True)
    count_row = lax.broadcasted_iota(jnp.int32, (TOKENS, TOKENS), 1).astype(jnp.float32)
    count_col = lax.broadcasted_iota(jnp.int32, (TOKENS, TOKENS), 0).astype(jnp.float32)
    turn = count_col == rank_row
    sorted_col = jnp.sum(jnp.where(turn, pos_row, 0.0), axis=1, keepdims=True)
    sorted_row = jnp.sum(jnp.where(count_row == rank_col, pos_col, 0.0), axis=0, keepdims=True)
    pos_stage[...] = jnp.broadcast_to(sorted_row, (8, TOKENS))
    run = ctx
    local(pos_stage, pos_out.at[run])
    pos_z = [remote(pos_stage, pos_out.at[run], z_up), remote(pos_stage, pos_out.at[run], z_down)]
    pos_y = remote(pos_stage, pos_out.at[run], opposite)
    turn = turn.astype(jnp.bfloat16)
    read.wait()
    sent_tokens = []
    for at in range(CHIPS):
        tok[at, :TOKENS] = jnp.dot(
            turn, stored[:, at * CHUNK : (at + 1) * CHUNK], preferred_element_type=jnp.float32
        ).astype(jnp.bfloat16)
        if at % 4 == 3:
            some = pl.ds(at - 3, 4)
            sent_tokens.append(remote(tok.at[some, pl.ds(0, TOKENS)], tok.at[some, pl.ds(TOKENS, TOKENS)], sibling))
    angle = sorted_col * freq[...]
    sign = jnp.where(lax.broadcasted_iota(jnp.int32, (1, HEAD_SIZE), 1) < HEAD_SIZE // 2, -1.0, 1.0)
    tables[0, 0] = jnp.cos(angle)
    tables[0, 1] = jnp.sin(angle) * sign
    sent_tables = remote(tables.at[0], tables.at[1], sibling)

    def neighbours_x(piece, row, with_y):
        (up, down), (up2, down2) = x1[piece]
        arrive(up, up2)
        second = [unit(piece, chip(left, row), core, x_up)]
        if with_y:
            y1[piece][3] = send_y(piece, chip(left, row))
        arrive(down, down2)
        second.append(unit(piece, chip(right, row), other, x_down))
        if with_y:
            y1[piece][1] = send_y(piece, chip(right, row))
        return second

    def across_x(piece, second):
        arrive(*second)
        y1[piece][2] = send_y(piece, chip(across))

    def rotate(value, which):
        return value * tables[which, 0] + pltpu.roll(value, HEAD_SIZE // 2, 1) * tables[which, 1]

    z1, y2, kv_sib, z2 = {}, {}, {}, {}

    def kv_block(head, of_run, part=slice(None)):
        return kv_out.at[head, part, of_run]

    def head_of(piece, whose):
        return (core if whose == 0 else other) * 2 + piece

    def send_kv(piece, whose):
        head = head_of(piece, whose)
        dst = kv_block(head, run)
        src = kv_stage.at[piece, 0] if whose == 0 else dst
        z1[piece, whose] = remote(src, dst, z_up), remote(src, dst, z_down)
        y2[piece, whose] = remote(src, dst, opposite)

    def pass_z(piece, whose, of_y, from_z1):
        head = head_of(piece, whose)
        arrive(*from_z1)
        low, high = pl.ds(0, BLOCKS // 2), pl.ds(BLOCKS // 2, BLOCKS // 2)
        a = kv_block(head, of_y * 4 + z_left, low)
        b = kv_block(head, of_y * 4 + z_right, high)
        return remote(a, a, z_up), remote(b, b, z_down)

    def pass_y(piece, whose):
        arrive(y2[piece, whose])
        ref = kv_block(head_of(piece, whose), (1 - y_hi) * 4 + z)
        return remote(ref, ref, z_up), remote(ref, ref, z_down)

    def finish_kv(piece):
        for s in range(2):
            rows = slice(s * TOKENS, (s + 1) * TOKENS)
            key = rotate(totals[piece][rows, :HEAD_SIZE], s).astype(jnp.bfloat16)
            value = totals[piece][rows, HEAD_SIZE:].astype(jnp.bfloat16)
            kv_stage[piece, s] = jnp.concatenate([key, value], axis=1).reshape(BLOCKS, PART, 2 * HEAD_SIZE)
        dst = kv_block(head_of(piece, 0), run)
        kv_sib[piece] = remote(kv_stage.at[piece, 1], dst, sibling)
        local(kv_stage.at[piece, 0], dst)
        send_kv(piece, 0)

    def second_kv(piece):
        arrive(kv_sib[piece])
        send_kv(piece, 1)

    def finish_q(piece):
        j = piece - 2
        for s in range(2):
            for g in range(4):
                rows = slice(s * TOKENS, (s + 1) * TOKENS)
                cols = slice(g * HEAD_SIZE, (g + 1) * HEAD_SIZE)
                q_stage[j, s, g] = rotate(totals[piece][rows, cols], s).astype(jnp.bfloat16)
        dst = q_out.at[pl.ds((core * 2 + j) * 4, 4)]
        local(q_stage.at[j, 0], dst)
        return remote(q_stage.at[j, 1], dst, sibling)

    second = neighbours_x(0, y_lo, True)
    arrive(*sent_tokens)
    add(0, me, True)
    add(0, chip(left))
    add(0, chip(right))
    across_x(0, second)
    second = neighbours_x(1, y_lo, True)
    start_x(2, me)
    finish_x(2, me)
    arrive(*sib[3])
    for copy in own[3]:
        copy.wait()
    q1_y = send_y(3, me)
    y1[2] = {0: send_y(2, me)}
    add(0, chip(across))
    arrive(*y1[0][0], *y1[0][1], *y1[0][3])
    add(0, chip(x, far))
    add(0, chip(left, far))
    add(0, chip(right, far))
    arrive(*y1[0][2])
    add(0, chip(across, far))
    arrive(sent_tables)
    finish_kv(0)
    pos_z2 = []
    arrive(*pos_z)
    ref = pos_out.at[y_hi * 4 + z_left]
    pos_z2.append(remote(ref, ref, z_up))
    arrive(pos_y)
    ref = pos_out.at[(1 - y_hi) * 4 + z]
    pos_far = [remote(ref, ref, z_up), remote(ref, ref, z_down)]

    across_x(1, second)
    add(1, me, True)
    add(1, chip(left))
    add(1, chip(right))
    add(1, chip(across))
    second_kv(0)
    arrive(*y1[1][0], *y1[1][1], *y1[1][3])
    add(1, chip(x, far))
    add(1, chip(left, far))
    add(1, chip(right, far))
    second = neighbours_x(2, y_lo, True)
    x1[3] = [send_x(3, me, core), send_x(3, me, other)]
    arrive(*y1[1][2])
    add(1, chip(across, far))
    finish_kv(1)
    z2[0, 0] = pass_z(0, 0, y_hi, z1[0, 0])
    z2[0, 1] = pass_z(0, 1, y_hi, z1[0, 1])
    second_kv(1)
    f1, f2 = {}, {}
    for whose in (0, 1):
        f1[0, whose] = pass_y(0, whose)

    across_x(2, second)
    add(2, me, True)
    add(2, chip(left))
    add(2, chip(right))
    add(2, chip(across))
    arrive(*pos_far)
    ref = pos_out.at[(1 - y_hi) * 4 + z_left]
    pos_far2 = remote(ref, ref, z_up)
    arrive(*q1_y)
    there = chip(x, far)
    second = neighbours_x(3, y_lo, False)
    x1[4] = [send_x(3, there, core), send_x(3, there, other)]
    for whose in (0, 1):
        f2[0, whose] = pass_z(0, whose, 1 - y_hi, f1[0, whose])
    for whose in (0, 1):
        z2[1, whose] = pass_z(1, whose, y_hi, z1[1, whose])
        f1[1, whose] = pass_y(1, whose)
    arrive(*y1[2][0], *y1[2][1], *y1[2][3])
    add(2, chip(x, far))
    add(2, chip(left, far))
    add(2, chip(right, far))
    arrive(*y1[2][2])
    add(2, chip(across, far))
    q_copies = [finish_q(2)]

    add(3, me, True)
    add(3, there)
    add(3, chip(left))
    add(3, chip(right))
    arrive(*second)
    add(3, chip(across))
    for whose in (0, 1):
        f2[1, whose] = pass_z(1, whose, 1 - y_hi, f1[1, whose])
    (up, down), (up2, down2) = x1[4]
    arrive(up, up2)
    second = [unit(3, chip(left, far), core, x_up)]
    arrive(down, down2)
    second.append(unit(3, chip(right, far), other, x_down))
    add(3, chip(left, far))
    add(3, chip(right, far))
    arrive(*second)
    add(3, chip(across, far))
    q_copies.append(finish_q(3))

    arrive(*pos_z2, pos_far2)
    for key in z2:
        arrive(*z2[key], *f2[key])
    arrive(*q_copies)
    for copy in copies:
        copy.wait_send()
    for copy in locals_[len(locals_) - 5 :]:
        copy.wait()


def projections(tokens, positions, freq, w_query, w_key, w_value):
    anywhere = pl.BlockSpec(memory_space=pl.ANY)
    vmem = pl.BlockSpec(memory_space=pltpu.VMEM)
    wide = 4 * HEAD_SIZE
    return pl.pallas_call(
        projection_kernel,
        out_shape=[
            jax.ShapeDtypeStruct((QUERY_HEADS, TOKENS, HEAD_SIZE), jnp.bfloat16),
            jax.ShapeDtypeStruct((KEY_VALUE_HEADS, BLOCKS, RUNS, PART, 2 * HEAD_SIZE), jnp.bfloat16),
            jax.ShapeDtypeStruct((RUNS, 8, TOKENS), jnp.float32),
        ],
        in_specs=[anywhere, vmem, vmem, anywhere, anywhere, anywhere],
        out_specs=[anywhere] * 3,
        scratch_shapes=[
            pltpu.VMEM((TOKENS, CHIPS * CHUNK), jnp.bfloat16),
            pltpu.VMEM((CHIPS, 2 * TOKENS, CHUNK), jnp.bfloat16),
            pltpu.VMEM((CHIPS, 2, ROWS, 2 * HEAD_SIZE), jnp.bfloat16),
            pltpu.VMEM((CHIPS, 2, ROWS, 2 * HEAD_SIZE), jnp.bfloat16),
            pltpu.VMEM((CHIPS, 2, ROWS, wide), jnp.bfloat16),
            pltpu.VMEM((CHIPS, 2, ROWS, wide), jnp.bfloat16),
            pltpu.VMEM((2 * TOKENS, 2 * HEAD_SIZE), jnp.float32),
            pltpu.VMEM((2 * TOKENS, 2 * HEAD_SIZE), jnp.float32),
            pltpu.VMEM((2 * TOKENS, wide), jnp.float32),
            pltpu.VMEM((2 * TOKENS, wide), jnp.float32),
            pltpu.VMEM((2, 2, TOKENS, HEAD_SIZE), jnp.float32),
            pltpu.VMEM((2, 2, BLOCKS, PART, 2 * HEAD_SIZE), jnp.bfloat16),
            pltpu.VMEM((2, 2, 4, TOKENS, HEAD_SIZE), jnp.bfloat16),
            pltpu.VMEM((8, TOKENS), jnp.float32),
            pltpu.SemaphoreType.DMA((16,)),
            pltpu.SemaphoreType.DMA((COPIES,)),
            pltpu.SemaphoreType.DMA((COPIES,)),
        ],
        compiler_params=pltpu.CompilerParams(
            collective_id=0, has_side_effects=True, vmem_limit_bytes=56 << 20
        ),
        cost_estimate=pl.CostEstimate(flops=10**10, bytes_accessed=2 * 10**7, transcendentals=10**5),
        name="projections",
    )(tokens, positions, freq, w_query, w_key, w_value)


def shards(tokens, positions, segment_ids, w_query, key_weight, value_weight):
    half = HEAD_SIZE // 2
    freq = 500000.0 ** (-jnp.arange(half, dtype=jnp.float32) / half)
    freq = jnp.concatenate([freq, freq])[None, :]
    query, kv, runs = projections(tokens[0], positions, freq, w_query, key_weight, value_weight)
    kv = kv.reshape(KEY_VALUE_HEADS, RUNS * TOKENS, 2 * HEAD_SIZE)
    return attention(query, kv, runs, positions, segment_ids)[None]


def solution(mesh):
    placed = (P("dp", "ctx", None), P("dp", "ctx"), P("dp", None), P("dp", None), P("dp", None), P("dp", None))
    return jax.shard_map(
        shards, mesh=mesh, in_specs=placed, out_specs=P("dp", "ctx", None), check_vma=False
    )
```

```python
import math

import jax
import jax.numpy as jnp
from jax import lax
from jax.experimental import pallas as pl
from jax.experimental.pallas import tpu as pltpu
from jax.sharding import PartitionSpec as P

QUERY_HEADS = 16
KEY_VALUE_HEADS = 4
HEAD_SIZE = 128
DOCS = 8


RUNS = 8
TOKENS = 384
KEY_BLOCK = 256
QUERY_TILE = 96
GROUP = 4
NEVER = -1e30


def attention_kernel(q_ref, kv_ref, runs_ref, stored_ref, seg_ref, out_ref, key_pos, top, total, summed, rows_done, qp, qs):
    part = KEY_BLOCK // RUNS
    blocks = TOKENS // part
    tiles = TOKENS // QUERY_TILE
    width = GROUP * QUERY_TILE
    factor = HEAD_SIZE ** -0.5 * math.log2(math.e)

    query_pos = runs_ref[lax.axis_index("ctx")][:1]
    seg = seg_ref[...]
    start = jnp.zeros_like(query_pos)
    for doc in range(1, DOCS):
        before = jnp.sum((seg < doc).astype(jnp.float32), axis=1, keepdims=True)
        start = jnp.where(before <= query_pos, jnp.maximum(start, before), start)

    runs = runs_ref[:, 0]
    for block in range(blocks):
        key_pos[block] = jnp.concatenate([runs[run : run + 1, block * part : (block + 1) * part] for run in range(RUNS)], axis=1)
    qp[...] = jnp.broadcast_to(jnp.broadcast_to(query_pos, (8, TOKENS)).T[:, :1], (TOKENS, 128))
    qs[...] = jnp.broadcast_to(jnp.broadcast_to(start, (8, TOKENS)).T[:, :1], (TOKENS, 128))

    lane = lax.broadcasted_iota(jnp.int32, (1, TOKENS), 1) % part
    lowest = jnp.where(lane == 0, jnp.min(runs, axis=0, keepdims=True), 1e9)
    highest = jnp.where(lane == part - 1, jnp.max(runs, axis=0, keepdims=True), 1e9)

    for tile in range(tiles):
        at = slice(tile * QUERY_TILE, (tile + 1) * QUERY_TILE)
        last = jnp.max(query_pos[:, at], axis=1, keepdims=True)
        first = jnp.min(start[:, at], axis=1, keepdims=True)
        begin = jnp.sum((highest < first).astype(jnp.int32))
        end = jnp.sum((lowest <= last).astype(jnp.int32))
        top[...] = jnp.full_like(top, NEVER)
        total[...] = jnp.zeros_like(total)
        summed[...] = jnp.zeros_like(summed)
        queries = [
            jnp.concatenate(
                [q_ref[head * GROUP + g, at] for g in range(GROUP)],
                axis=0,
            )
            for head in range(KEY_VALUE_HEADS)
        ]

        def one_block(block, carry):
            rows = pl.ds(pl.multiple_of(block * KEY_BLOCK, KEY_BLOCK), KEY_BLOCK)
            pos = key_pos[block]
            q_at = jnp.concatenate([qp[at]] * (KEY_BLOCK // 128), axis=1)
            s_at = jnp.concatenate([qs[at]] * (KEY_BLOCK // 128), axis=1)
            visible = (pos <= q_at) & (pos >= s_at)
            visible = jnp.concatenate([visible] * GROUP, axis=0)
            scores = [lax.dot_general(queries[head], kv_ref[head, rows, :HEAD_SIZE], (((1,), (1,)), ((), ())), preferred_element_type=jnp.float32) for head in range(KEY_VALUE_HEADS)]
            weights=[]; fades=[]
            for head in range(KEY_VALUE_HEADS):
                SC = scores[head]
                score = jnp.where(visible, SC, -jnp.inf)
                old = top[head]
                new = jnp.maximum(old, jnp.max(score, axis=1, keepdims=True))
                wide = jnp.concatenate([new] * (KEY_BLOCK // 128), axis=1)
                weight = jnp.exp2((score - wide) * factor)
                fade = jnp.exp2((old - new) * factor)
                top[head] = new
                total[head] = total[head] * fade + weight[:, :128] + weight[:, 128:]
                weight = weight.astype(jnp.bfloat16)
                weights.append(weight); fades.append(fade)
            for head in range(KEY_VALUE_HEADS):
                added = jnp.dot(weights[head], kv_ref[head, rows, HEAD_SIZE:], preferred_element_type=jnp.float32)
                summed[head] = summed[head] * fades[head] + added
            return carry

        lax.fori_loop(begin, end, one_block, 0)
        for head in range(KEY_VALUE_HEADS):
            result = (summed[head] / jnp.sum(total[head], axis=1, keepdims=True)).astype(jnp.bfloat16)
            for g in range(GROUP):
                rows_done[head * GROUP + g, at] = result[g * QUERY_TILE : (g + 1) * QUERY_TILE]

    stored = jnp.broadcast_to(stored_ref[...].astype(jnp.float32), (8, TOKENS)).T[:, :1]
    turn = (stored == query_pos).astype(jnp.bfloat16)
    for head in range(QUERY_HEADS):
        out_ref[:, head * HEAD_SIZE : (head + 1) * HEAD_SIZE] = lax.dot_general(
            turn, rows_done[head], (((1,), (0,)), ((), ())), preferred_element_type=jnp.float32
        ).astype(jnp.bfloat16)


def attention(query, kv, runs, stored, seg):
    part = KEY_BLOCK // RUNS
    width = GROUP * QUERY_TILE
    return pl.pallas_call(
        attention_kernel,
        out_shape=jax.ShapeDtypeStruct((TOKENS, QUERY_HEADS * HEAD_SIZE), jnp.bfloat16),
        in_specs=[pl.BlockSpec(memory_space=pltpu.VMEM)] * 5,
        out_specs=pl.BlockSpec(memory_space=pltpu.VMEM),
        scratch_shapes=[
            pltpu.VMEM((TOKENS // part, 1, KEY_BLOCK), jnp.float32),
            pltpu.VMEM((KEY_VALUE_HEADS, width, 128), jnp.float32),
            pltpu.VMEM((KEY_VALUE_HEADS, width, 128), jnp.float32),
            pltpu.VMEM((KEY_VALUE_HEADS, width, HEAD_SIZE), jnp.float32),
            pltpu.VMEM((QUERY_HEADS, TOKENS, HEAD_SIZE), jnp.bfloat16),
            pltpu.VMEM((TOKENS, 128), jnp.float32),
            pltpu.VMEM((TOKENS, 128), jnp.float32),
        ],
        compiler_params=pltpu.CompilerParams(vmem_limit_bytes=56 << 20),
        cost_estimate=pl.CostEstimate(flops=5 * 10**9, bytes_accessed=11 * 10**6, transcendentals=10**7),
        name="attention",
    )(query, kv, runs, stored, seg)


ROWS = 256
CHIPS = 8
CHUNK = 2 * ROWS
COPIES = 144
PART = KEY_BLOCK // RUNS
BLOCKS = TOKENS // PART


def projection_kernel(
    tokens, positions, freq, w_query, w_key, w_value,
    q_out, kv_out, pos_out,
    stored, tok, weights_a, weights_b, weights_c, weights_d,
    acc_a, acc_b, acc_c, acc_d, tables, kv_stage, q_stage, pos_stage,
    local_sem, send_sem, recv_sem,
):
    dp, ctx = lax.axis_index("dp"), lax.axis_index("ctx")
    core, x, y_lo = dp % 2, (dp // 2) % 4, dp // 8
    y_hi, z = ctx // 4, ctx % 4
    other = 1 - core

    def device(core=core, x=x, y_lo=y_lo, y_hi=y_hi, z=z):
        return ((y_lo * 4 + x) * 2 + core, y_hi * 4 + z)

    right, left, across = (x + 1) % 4, (x + 3) % 4, (x + 2) % 4
    z_right, z_left = (z + 1) % 4, (z + 3) % 4
    far = 1 - y_lo
    y_up = device(y_lo=far, y_hi=(y_hi + y_lo) % 2)
    y_down = device(y_lo=far, y_hi=(y_hi + far) % 2)
    x_up, x_down = device(x=right), device(x=left)
    z_up, z_down = device(z=z_right), device(z=z_left)
    sibling = device(core=other)
    opposite = device(y_hi=1 - y_hi)

    locals_, copies = [], []

    def local(src, dst):
        copy = pltpu.make_async_copy(src, dst, local_sem.at[len(locals_)])
        locals_.append(copy)
        copy.start()
        return copy

    def remote(src, dst, to):
        at = len(copies)
        copy = pltpu.make_async_remote_copy(
            src_ref=src, dst_ref=dst, send_sem=send_sem.at[at], recv_sem=recv_sem.at[at],
            device_id=to, device_id_type=pl.DeviceIdType.MESH,
        )
        copies.append(copy)
        copy.start()
        return copy

    def chip(x, row=y_lo):
        return row * 4 + x

    def columns(ref, start, size):
        return ref.at[:, pl.ds(pl.multiple_of(start, size), size)]

    me = chip(x)
    half = HEAD_SIZE
    buffers = (weights_a, weights_b, weights_c, weights_d)
    totals = (acc_a, acc_b, acc_c, acc_d)

    def sources(piece, of_core):
        if piece < 2:
            start = (of_core * 2 + piece) * half
            return [(columns(w_key, start, half), slice(0, half)), (columns(w_value, start, half), slice(half, 2 * half))]
        start = (of_core * 2 + piece - 2) * 4 * half
        return [(columns(w_query, start, 4 * half), slice(0, 4 * half))]

    own = [[local(src, buffers[p].at[me, core, :, to]) for src, to in sources(p, core)] for p in (0, 1)]
    read = local(tokens, stored)
    own += [[local(src, buffers[p].at[me, core, :, to]) for src, to in sources(p, core)] for p in (2, 3)]

    barrier = pltpu.get_barrier_semaphore()
    partners = (sibling, x_up, x_down, y_up, y_down, z_up, z_down, opposite)
    for partner in partners:
        pl.semaphore_signal(barrier, inc=1, device_id=partner, device_id_type=pl.DeviceIdType.MESH)
    pl.semaphore_wait(barrier, len(partners))

    def to_sibling(piece):
        return [remote(src, buffers[piece].at[me, core, :, to], sibling) for src, to in sources(piece, other)]

    mine = pl.ds(pl.multiple_of((z % 2) * (ROWS // 2), ROWS // 2), ROWS // 2)

    def unit(piece, at, row, to):
        ref = buffers[piece].at[at, row, mine] if piece == 0 else buffers[piece].at[at, row]
        return remote(ref, ref, to)

    def send_z(at):
        return unit(0, at, core, z_up), unit(0, at, other, z_down)

    def send_x(piece, at, row):
        return unit(piece, at, row, x_up), unit(piece, at, row, x_down)

    def send_y(piece, at):
        return unit(piece, at, core, y_up), unit(piece, at, other, y_down)

    def arrive(*some):
        for copy in some:
            copy.wait_recv()

    def add(piece, at, first=False):
        weights = buffers[piece][at]
        product = jnp.dot(
            tok[at], weights.reshape(CHUNK, weights.shape[-1]), preferred_element_type=jnp.float32
        )
        if first:
            totals[piece][...] = product
        else:
            totals[piece][...] += product

    sib, x1, y1, by_z = {}, {}, {}, []

    def start(piece):
        for copy in own[piece]:
            copy.wait()
        x1[piece] = [send_x(piece, me, core)]
        up = unit(piece, me, core, y_up)
        arrive(*sib[piece])
        x1[piece].append(send_x(piece, me, other))
        y1[piece] = {0: (up, unit(piece, me, other, y_down))}

    sib[0] = to_sibling(0)
    start(0)
    sib[1] = to_sibling(1)

    pos_row = positions[...].astype(jnp.float32)
    pos_col = jnp.broadcast_to(pos_row, (8, TOKENS)).T[:, :1]
    rank_row = jnp.sum((pos_col < pos_row).astype(jnp.float32), axis=0, keepdims=True)
    rank_col = jnp.sum((pos_row < pos_col).astype(jnp.float32), axis=1, keepdims=True)
    count_row = lax.broadcasted_iota(jnp.int32, (TOKENS, TOKENS), 1).astype(jnp.float32)
    count_col = lax.broadcasted_iota(jnp.int32, (TOKENS, TOKENS), 0).astype(jnp.float32)
    turn = count_col == rank_row
    sorted_col = jnp.sum(jnp.where(turn, pos_row, 0.0), axis=1, keepdims=True)
    sorted_row = jnp.sum(jnp.where(count_row == rank_col, pos_col, 0.0), axis=0, keepdims=True)
    pos_stage[...] = jnp.broadcast_to(sorted_row, (8, TOKENS))
    run = ctx
    local(pos_stage, pos_out.at[run])
    pos_z = [remote(pos_stage, pos_out.at[run], z_up), remote(pos_stage, pos_out.at[run], z_down)]
    pos_y = remote(pos_stage, pos_out.at[run], opposite)
    turn = turn.astype(jnp.bfloat16)
    read.wait()
    sent_tokens = []
    for at in range(CHIPS):
        tok[at, :TOKENS] = jnp.dot(
            turn, stored[:, at * CHUNK : (at + 1) * CHUNK], preferred_element_type=jnp.float32
        ).astype(jnp.bfloat16)
        if at % 4 == 3:
            some = pl.ds(at - 3, 4)
            sent_tokens.append(remote(tok.at[some, pl.ds(0, TOKENS)], tok.at[some, pl.ds(TOKENS, TOKENS)], sibling))
    angle = sorted_col * freq[...]
    sign = jnp.where(lax.broadcasted_iota(jnp.int32, (1, HEAD_SIZE), 1) < HEAD_SIZE // 2, -1.0, 1.0)
    tables[0, 0] = jnp.cos(angle)
    tables[0, 1] = jnp.sin(angle) * sign
    sent_tables = remote(tables.at[0], tables.at[1], sibling)

    def neighbours_x(piece, row, with_y):
        (up, down), (up2, down2) = x1[piece]
        arrive(up, up2)
        second = [unit(piece, chip(left, row), core, x_up)]
        if with_y:
            y1[piece][3] = send_y(piece, chip(left, row))
        if piece == 0:
            by_z.append(send_z(chip(left)))
        arrive(down, down2)
        second.append(unit(piece, chip(right, row), other, x_down))
        if with_y:
            y1[piece][1] = send_y(piece, chip(right, row))
        if piece == 0:
            by_z.append(send_z(chip(right)))
        return second

    def across_x(piece, second):
        arrive(*second)
        y1[piece][2] = send_y(piece, chip(across))
        if piece == 0:
            by_z.append(send_z(chip(across)))

    def rotate(value, which):
        return value * tables[which, 0] + pltpu.roll(value, HEAD_SIZE // 2, 1) * tables[which, 1]

    z1, y2, kv_sib, z2 = {}, {}, {}, {}

    def kv_block(head, of_run, part=slice(None)):
        return kv_out.at[head, part, of_run]

    def head_of(piece, whose):
        return (core if whose == 0 else other) * 2 + piece

    def send_kv(piece, whose):
        head = head_of(piece, whose)
        dst = kv_block(head, run)
        src = kv_stage.at[piece, 0] if whose == 0 else dst
        z1[piece, whose] = remote(src, dst, z_up), remote(src, dst, z_down)
        y2[piece, whose] = remote(src, dst, opposite)

    def pass_z(piece, whose, of_y, from_z1):
        head = head_of(piece, whose)
        arrive(*from_z1)
        low, high = pl.ds(0, BLOCKS // 2), pl.ds(BLOCKS // 2, BLOCKS // 2)
        a = kv_block(head, of_y * 4 + z_left, low)
        b = kv_block(head, of_y * 4 + z_right, high)
        return remote(a, a, z_up), remote(b, b, z_down)

    def pass_y(piece, whose):
        arrive(y2[piece, whose])
        ref = kv_block(head_of(piece, whose), (1 - y_hi) * 4 + z)
        return remote(ref, ref, z_up), remote(ref, ref, z_down)

    def finish_kv(piece):
        for s in range(2):
            rows = slice(s * TOKENS, (s + 1) * TOKENS)
            key = rotate(totals[piece][rows, :HEAD_SIZE], s).astype(jnp.bfloat16)
            value = totals[piece][rows, HEAD_SIZE:].astype(jnp.bfloat16)
            kv_stage[piece, s] = jnp.concatenate([key, value], axis=1).reshape(BLOCKS, PART, 2 * HEAD_SIZE)
        dst = kv_block(head_of(piece, 0), run)
        kv_sib[piece] = remote(kv_stage.at[piece, 1], dst, sibling)
        local(kv_stage.at[piece, 0], dst)
        send_kv(piece, 0)

    def second_kv(piece):
        arrive(kv_sib[piece])
        send_kv(piece, 1)

    def finish_q(piece):
        j = piece - 2
        for s in range(2):
            for g in range(4):
                rows = slice(s * TOKENS, (s + 1) * TOKENS)
                cols = slice(g * HEAD_SIZE, (g + 1) * HEAD_SIZE)
                q_stage[j, s, g] = rotate(totals[piece][rows, cols], s).astype(jnp.bfloat16)
        dst = q_out.at[pl.ds((core * 2 + j) * 4, 4)]
        local(q_stage.at[j, 0], dst)
        return remote(q_stage.at[j, 1], dst, sibling)

    second = neighbours_x(0, y_lo, True)
    start(1)
    sib[2], sib[3] = to_sibling(2), to_sibling(3)
    across_x(0, second)
    for which, there in ((0, x), (3, left), (1, right)):
        arrive(*y1[0][which])
        by_z.append(send_z(chip(there, far)))
    arrive(*sent_tokens)
    add(0, me, True)
    for at, there in enumerate((left, right, across)):
        arrive(*by_z[at])
        add(0, chip(there))
    arrive(*y1[0][2])
    by_z.append(send_z(chip(across, far)))
    second = neighbours_x(1, y_lo, True)
    start(2)
    for at, there in enumerate((x, left, right, across)):
        arrive(*by_z[at + 3])
        add(0, chip(there, far))
    arrive(sent_tables)
    finish_kv(0)
    across_x(1, second)
    second_kv(0)

    for copy in own[3]:
        copy.wait()
    arrive(*sib[3])
    q1_y = send_y(3, me)
    add(1, me, True)
    add(1, chip(left))
    add(1, chip(right))
    add(1, chip(across))
    second = neighbours_x(2, y_lo, True)
    x1[3] = [send_x(3, me, core), send_x(3, me, other)]
    pos_z2 = []
    arrive(*pos_z)
    ref = pos_out.at[y_hi * 4 + z_left]
    pos_z2.append(remote(ref, ref, z_up))
    arrive(pos_y)
    ref = pos_out.at[(1 - y_hi) * 4 + z]
    pos_far = [remote(ref, ref, z_up), remote(ref, ref, z_down)]
    z2[0, 0] = pass_z(0, 0, y_hi, z1[0, 0])
    z2[0, 1] = pass_z(0, 1, y_hi, z1[0, 1])
    f1, f2 = {}, {}
    for whose in (0, 1):
        f1[0, whose] = pass_y(0, whose)
    arrive(*y1[1][0], *y1[1][1], *y1[1][3])
    add(1, chip(x, far))
    add(1, chip(left, far))
    add(1, chip(right, far))
    arrive(*y1[1][2])
    add(1, chip(across, far))
    finish_kv(1)
    second_kv(1)

    across_x(2, second)
    add(2, me, True)
    add(2, chip(left))
    add(2, chip(right))
    add(2, chip(across))
    arrive(*pos_far)
    ref = pos_out.at[(1 - y_hi) * 4 + z_left]
    pos_far2 = remote(ref, ref, z_up)
    arrive(*q1_y)
    there = chip(x, far)
    second = neighbours_x(3, y_lo, False)
    x1[4] = [send_x(3, there, core), send_x(3, there, other)]
    for whose in (0, 1):
        f2[0, whose] = pass_z(0, whose, 1 - y_hi, f1[0, whose])
    for whose in (0, 1):
        z2[1, whose] = pass_z(1, whose, y_hi, z1[1, whose])
        f1[1, whose] = pass_y(1, whose)
    arrive(*y1[2][0], *y1[2][1], *y1[2][3])
    add(2, chip(x, far))
    add(2, chip(left, far))
    add(2, chip(right, far))
    arrive(*y1[2][2])
    add(2, chip(across, far))
    q_copies = [finish_q(2)]

    add(3, me, True)
    add(3, there)
    add(3, chip(left))
    add(3, chip(right))
    arrive(*second)
    add(3, chip(across))
    for whose in (0, 1):
        f2[1, whose] = pass_z(1, whose, 1 - y_hi, f1[1, whose])
    (up, down), (up2, down2) = x1[4]
    arrive(up, up2)
    second = [unit(3, chip(left, far), core, x_up)]
    arrive(down, down2)
    second.append(unit(3, chip(right, far), other, x_down))
    add(3, chip(left, far))
    add(3, chip(right, far))
    arrive(*second)
    add(3, chip(across, far))
    q_copies.append(finish_q(3))

    arrive(*pos_z2, pos_far2)
    for key in z2:
        arrive(*z2[key], *f2[key])
    arrive(*q_copies)
    for copy in copies:
        copy.wait_send()
    for copy in locals_[len(locals_) - 5 :]:
        copy.wait()


def projections(tokens, positions, freq, w_query, w_key, w_value):
    anywhere = pl.BlockSpec(memory_space=pl.ANY)
    vmem = pl.BlockSpec(memory_space=pltpu.VMEM)
    wide = 4 * HEAD_SIZE
    return pl.pallas_call(
        projection_kernel,
        out_shape=[
            jax.ShapeDtypeStruct((QUERY_HEADS, TOKENS, HEAD_SIZE), jnp.bfloat16),
            jax.ShapeDtypeStruct((KEY_VALUE_HEADS, BLOCKS, RUNS, PART, 2 * HEAD_SIZE), jnp.bfloat16),
            jax.ShapeDtypeStruct((RUNS, 8, TOKENS), jnp.float32),
        ],
        in_specs=[anywhere, vmem, vmem, anywhere, anywhere, anywhere],
        out_specs=[anywhere] * 3,
        scratch_shapes=[
            pltpu.VMEM((TOKENS, CHIPS * CHUNK), jnp.bfloat16),
            pltpu.VMEM((CHIPS, 2 * TOKENS, CHUNK), jnp.bfloat16),
            pltpu.VMEM((CHIPS, 2, ROWS, 2 * HEAD_SIZE), jnp.bfloat16),
            pltpu.VMEM((CHIPS, 2, ROWS, 2 * HEAD_SIZE), jnp.bfloat16),
            pltpu.VMEM((CHIPS, 2, ROWS, wide), jnp.bfloat16),
            pltpu.VMEM((CHIPS, 2, ROWS, wide), jnp.bfloat16),
            pltpu.VMEM((2 * TOKENS, 2 * HEAD_SIZE), jnp.float32),
            pltpu.VMEM((2 * TOKENS, 2 * HEAD_SIZE), jnp.float32),
            pltpu.VMEM((2 * TOKENS, wide), jnp.float32),
            pltpu.VMEM((2 * TOKENS, wide), jnp.float32),
            pltpu.VMEM((2, 2, TOKENS, HEAD_SIZE), jnp.float32),
            pltpu.VMEM((2, 2, BLOCKS, PART, 2 * HEAD_SIZE), jnp.bfloat16),
            pltpu.VMEM((2, 2, 4, TOKENS, HEAD_SIZE), jnp.bfloat16),
            pltpu.VMEM((8, TOKENS), jnp.float32),
            pltpu.SemaphoreType.DMA((16,)),
            pltpu.SemaphoreType.DMA((COPIES,)),
            pltpu.SemaphoreType.DMA((COPIES,)),
        ],
        compiler_params=pltpu.CompilerParams(
            collective_id=0, has_side_effects=True, vmem_limit_bytes=56 << 20
        ),
        cost_estimate=pl.CostEstimate(flops=10**10, bytes_accessed=2 * 10**7, transcendentals=10**5),
        name="projections",
    )(tokens, positions, freq, w_query, w_key, w_value)


def shards(tokens, positions, segment_ids, w_query, key_weight, value_weight):
    half = HEAD_SIZE // 2
    freq = 500000.0 ** (-jnp.arange(half, dtype=jnp.float32) / half)
    freq = jnp.concatenate([freq, freq])[None, :]
    query, kv, runs = projections(tokens[0], positions, freq, w_query, key_weight, value_weight)
    kv = kv.reshape(KEY_VALUE_HEADS, RUNS * TOKENS, 2 * HEAD_SIZE)
    return attention(query, kv, runs, positions, segment_ids)[None]


def solution(mesh):
    placed = (P("dp", "ctx", None), P("dp", "ctx"), P("dp", None), P("dp", None), P("dp", None), P("dp", None))
    return jax.shard_map(
        shards, mesh=mesh, in_specs=placed, out_specs=P("dp", "ctx", None), check_vma=False
    )
```

```python
import math

import jax
import jax.numpy as jnp
from jax import lax
from jax.experimental import pallas as pl
from jax.experimental.pallas import tpu as pltpu
from jax.sharding import PartitionSpec as P

QUERY_HEADS = 16
KEY_VALUE_HEADS = 4
HEAD_SIZE = 128
DOCS = 8


RUNS = 8
TOKENS = 384
KEY_BLOCK = 256
QUERY_TILE = 96
GROUP = 4
NEVER = -1e30


def attention_kernel(
    q_hbm, kv_hbm, runs_ref, stored_ref, seg_ref, out_ref,
    q_ref, kv_ref, key_pos, query_at, start_at, top, total, summed, rows_done, sem,
):
    part = KEY_BLOCK // RUNS
    blocks = TOKENS // part
    tiles = TOKENS // QUERY_TILE
    factor = HEAD_SIZE ** -0.5 * math.log2(math.e)
    loads = [pltpu.make_async_copy(q_hbm, q_ref, sem.at[0]), pltpu.make_async_copy(kv_hbm, kv_ref, sem.at[1])]
    for load in loads:
        load.start()

    query_pos = runs_ref[lax.axis_index("ctx")][:1]
    seg = seg_ref[...]
    start = jnp.zeros_like(query_pos)
    for doc in range(1, DOCS):
        before = jnp.sum((seg < doc).astype(jnp.float32), axis=1, keepdims=True)
        start = jnp.where(before <= query_pos, jnp.maximum(start, before), start)

    runs = runs_ref[:, 0]
    for block in range(blocks):
        at = slice(block * part, (block + 1) * part)
        key_pos[block] = jnp.concatenate([runs[run : run + 1, at] for run in range(RUNS)], axis=1)
    query_at[...] = jnp.broadcast_to(jnp.broadcast_to(query_pos, (8, TOKENS)).T[:, :1], (TOKENS, 128))
    start_at[...] = jnp.broadcast_to(jnp.broadcast_to(start, (8, TOKENS)).T[:, :1], (TOKENS, 128))

    lane = lax.broadcasted_iota(jnp.int32, (1, TOKENS), 1) % part
    lowest = jnp.where(lane == 0, jnp.min(runs, axis=0, keepdims=True), 1e9)
    highest = jnp.where(lane == part - 1, jnp.max(runs, axis=0, keepdims=True), 1e9)
    ranges = []
    for tile in range(tiles):
        at = slice(tile * QUERY_TILE, (tile + 1) * QUERY_TILE)
        last = jnp.max(query_pos[:, at], axis=1, keepdims=True)
        first = jnp.min(start[:, at], axis=1, keepdims=True)
        ranges.append((jnp.sum((highest < first).astype(jnp.int32)), jnp.sum((lowest <= last).astype(jnp.int32))))
    for load in loads:
        load.wait()

    for tile in range(tiles):
        at = slice(tile * QUERY_TILE, (tile + 1) * QUERY_TILE)
        begin, end = ranges[tile]
        top[...] = jnp.full_like(top, NEVER)
        total[...] = jnp.zeros_like(total)
        summed[...] = jnp.zeros_like(summed)
        queries = [
            jnp.concatenate([q_ref[head * GROUP + g, at] for g in range(GROUP)], axis=0)
            for head in range(KEY_VALUE_HEADS)
        ]

        def step(block, count):
            rows = pl.ds(pl.multiple_of(block * KEY_BLOCK, KEY_BLOCK), count * KEY_BLOCK)
            pos = jnp.concatenate([key_pos[block + i] for i in range(count)], axis=1)
            lanes = count * KEY_BLOCK // 128
            visible = (pos <= jnp.concatenate([query_at[at]] * lanes, axis=1)) & (
                pos >= jnp.concatenate([start_at[at]] * lanes, axis=1)
            )
            visible = jnp.concatenate([visible] * GROUP, axis=0)
            scores = [
                lax.dot_general(
                    queries[head], kv_ref[head, rows, :HEAD_SIZE], (((1,), (1,)), ((), ())),
                    preferred_element_type=jnp.float32,
                )
                for head in range(KEY_VALUE_HEADS)
            ]
            weights, fades = [], []
            for head in range(KEY_VALUE_HEADS):
                score = jnp.where(visible, scores[head], -jnp.inf)
                old = top[head]
                new = jnp.maximum(old, jnp.max(score, axis=1, keepdims=True))
                weight = jnp.exp2((score - jnp.concatenate([new] * lanes, axis=1)) * factor)
                fade = jnp.exp2((old - new) * factor)
                top[head] = new
                total[head] = total[head] * fade + sum(weight[:, i * 128 : (i + 1) * 128] for i in range(lanes))
                weights.append(weight.astype(jnp.bfloat16))
                fades.append(fade)
            for head in range(KEY_VALUE_HEADS):
                added = jnp.dot(weights[head], kv_ref[head, rows, HEAD_SIZE:], preferred_element_type=jnp.float32)
                summed[head] = summed[head] * fades[head] + added

        pairs = (end - begin) // 2

        @pl.loop(0, pairs)
        def _(pair):
            step(begin + 2 * pair, 2)

        @pl.loop(begin + 2 * pairs, end)
        def _(block):
            step(block, 1)

        for head in range(KEY_VALUE_HEADS):
            result = (summed[head] / jnp.sum(total[head], axis=1, keepdims=True)).astype(jnp.bfloat16)
            for g in range(GROUP):
                cols = slice((head * GROUP + g) * HEAD_SIZE, (head * GROUP + g + 1) * HEAD_SIZE)
                rows_done[at, cols] = result[g * QUERY_TILE : (g + 1) * QUERY_TILE]

    stored = jnp.broadcast_to(stored_ref[...].astype(jnp.float32), (8, TOKENS)).T[:, :1]
    turn = (stored == query_pos).astype(jnp.bfloat16)
    wide = 4 * HEAD_SIZE
    for at in range(0, QUERY_HEADS * HEAD_SIZE, wide):
        out_ref[:, at : at + wide] = jnp.dot(
            turn, rows_done[:, at : at + wide], preferred_element_type=jnp.float32
        ).astype(jnp.bfloat16)


def attention(query, kv, runs, stored, seg):
    part = KEY_BLOCK // RUNS
    width = GROUP * QUERY_TILE
    vmem = pl.BlockSpec(memory_space=pltpu.VMEM)
    anywhere = pl.BlockSpec(memory_space=pl.ANY)
    return pl.pallas_call(
        attention_kernel,
        out_shape=jax.ShapeDtypeStruct((TOKENS, QUERY_HEADS * HEAD_SIZE), jnp.bfloat16),
        in_specs=[anywhere, anywhere, vmem, vmem, vmem],
        out_specs=vmem,
        scratch_shapes=[
            pltpu.VMEM((QUERY_HEADS, TOKENS, HEAD_SIZE), jnp.bfloat16),
            pltpu.VMEM((KEY_VALUE_HEADS, RUNS * TOKENS, 2 * HEAD_SIZE), jnp.bfloat16),
            pltpu.VMEM((TOKENS // part, 1, KEY_BLOCK), jnp.float32),
            pltpu.VMEM((TOKENS, 128), jnp.float32),
            pltpu.VMEM((TOKENS, 128), jnp.float32),
            pltpu.VMEM((KEY_VALUE_HEADS, width, 128), jnp.float32),
            pltpu.VMEM((KEY_VALUE_HEADS, width, 128), jnp.float32),
            pltpu.VMEM((KEY_VALUE_HEADS, width, HEAD_SIZE), jnp.float32),
            pltpu.VMEM((TOKENS, QUERY_HEADS * HEAD_SIZE), jnp.bfloat16),
            pltpu.SemaphoreType.DMA((2,)),
        ],
        compiler_params=pltpu.CompilerParams(vmem_limit_bytes=56 << 20),
        cost_estimate=pl.CostEstimate(flops=5 * 10**9, bytes_accessed=11 * 10**6, transcendentals=10**7),
        name="attention",
    )(query, kv, runs, stored, seg)


ROWS = 256
CHIPS = 8
CHUNK = 2 * ROWS
COPIES = 144
PART = KEY_BLOCK // RUNS
BLOCKS = TOKENS // PART


def projection_kernel(
    tokens, positions, freq, w_query, w_key, w_value,
    q_out, kv_out, pos_out,
    stored, tok, weights_a, weights_b, weights_c, weights_d,
    acc_a, acc_b, acc_c, acc_d, tables, kv_stage, q_stage, pos_stage,
    local_sem, send_sem, recv_sem,
):
    dp, ctx = lax.axis_index("dp"), lax.axis_index("ctx")
    core, x, y_lo = dp % 2, (dp // 2) % 4, dp // 8
    y_hi, z = ctx // 4, ctx % 4
    other = 1 - core

    def device(core=core, x=x, y_lo=y_lo, y_hi=y_hi, z=z):
        return ((y_lo * 4 + x) * 2 + core, y_hi * 4 + z)

    right, left, across = (x + 1) % 4, (x + 3) % 4, (x + 2) % 4
    z_right, z_left = (z + 1) % 4, (z + 3) % 4
    far = 1 - y_lo
    y_up = device(y_lo=far, y_hi=(y_hi + y_lo) % 2)
    y_down = device(y_lo=far, y_hi=(y_hi + far) % 2)
    x_up, x_down = device(x=right), device(x=left)
    z_up, z_down = device(z=z_right), device(z=z_left)
    sibling = device(core=other)
    opposite = device(y_hi=1 - y_hi)

    locals_, copies = [], []

    def local(src, dst):
        copy = pltpu.make_async_copy(src, dst, local_sem.at[len(locals_)])
        locals_.append(copy)
        copy.start()
        return copy

    def remote(src, dst, to):
        at = len(copies)
        copy = pltpu.make_async_remote_copy(
            src_ref=src, dst_ref=dst, send_sem=send_sem.at[at], recv_sem=recv_sem.at[at],
            device_id=to, device_id_type=pl.DeviceIdType.MESH,
        )
        copies.append(copy)
        copy.start()
        return copy

    def chip(x, row=y_lo):
        return row * 4 + x

    def columns(ref, start, size):
        return ref.at[:, pl.ds(pl.multiple_of(start, size), size)]

    me = chip(x)
    half = HEAD_SIZE
    buffers = (weights_a, weights_b, weights_c, weights_d)
    totals = (acc_a, acc_b, acc_c, acc_d)

    def sources(piece, of_core):
        if piece < 2:
            start = (of_core * 2 + piece) * half
            return [(columns(w_key, start, half), slice(0, half)), (columns(w_value, start, half), slice(half, 2 * half))]
        start = (of_core * 2 + piece - 2) * 4 * half
        return [(columns(w_query, start, 4 * half), slice(0, 4 * half))]

    own = [[local(src, buffers[p].at[me, core, :, to]) for src, to in sources(p, core)] for p in (0, 1)]
    read = local(tokens, stored)
    own += [[local(src, buffers[p].at[me, core, :, to]) for src, to in sources(p, core)] for p in (2, 3)]

    barrier = pltpu.get_barrier_semaphore()
    partners = (sibling, x_up, x_down, y_up, y_down, z_up, z_down, opposite)
    for partner in partners:
        pl.semaphore_signal(barrier, inc=1, device_id=partner, device_id_type=pl.DeviceIdType.MESH)

    pos_row = positions[...].astype(jnp.float32)
    pos_col = jnp.broadcast_to(pos_row, (8, TOKENS)).T[:, :1]
    rank_row = jnp.sum((pos_col < pos_row).astype(jnp.float32), axis=0, keepdims=True)
    rank_col = jnp.sum((pos_row < pos_col).astype(jnp.float32), axis=1, keepdims=True)
    count_row = lax.broadcasted_iota(jnp.int32, (TOKENS, TOKENS), 1).astype(jnp.float32)
    count_col = lax.broadcasted_iota(jnp.int32, (TOKENS, TOKENS), 0).astype(jnp.float32)
    turn = count_col == rank_row
    sorted_col = jnp.sum(jnp.where(turn, pos_row, 0.0), axis=1, keepdims=True)
    sorted_row = jnp.sum(jnp.where(count_row == rank_col, pos_col, 0.0), axis=0, keepdims=True)
    pos_stage[...] = jnp.broadcast_to(sorted_row, (8, TOKENS))
    turn = turn.astype(jnp.bfloat16)
    run = ctx

    pl.semaphore_wait(barrier, len(partners))

    def to_sibling(piece):
        return [remote(src, buffers[piece].at[me, core, :, to], sibling) for src, to in sources(piece, other)]

    mine = pl.ds(pl.multiple_of((z % 2) * (ROWS // 2), ROWS // 2), ROWS // 2)

    def unit(piece, at, row, to):
        ref = buffers[piece].at[at, row, mine] if piece == 0 else buffers[piece].at[at, row]
        return remote(ref, ref, to)

    def send_z(at):
        return unit(0, at, core, z_up), unit(0, at, other, z_down)

    def send_x(piece, at, row):
        return unit(piece, at, row, x_up), unit(piece, at, row, x_down)

    def send_y(piece, at):
        return unit(piece, at, core, y_up), unit(piece, at, other, y_down)

    def arrive(*some):
        for copy in some:
            copy.wait_recv()

    def add(piece, at, first=False):
        weights = buffers[piece][at]
        product = jnp.dot(
            tok[at], weights.reshape(CHUNK, weights.shape[-1]), preferred_element_type=jnp.float32
        )
        if first:
            totals[piece][...] = product
        else:
            totals[piece][...] += product


    def sort_tokens(first):
        for at in range(first, first + 4):
            tok[at, :TOKENS] = jnp.dot(
                turn, stored[:, at * CHUNK : (at + 1) * CHUNK], preferred_element_type=jnp.float32
            ).astype(jnp.bfloat16)
        some = pl.ds(first, 4)
        return remote(tok.at[some, pl.ds(0, TOKENS)], tok.at[some, pl.ds(TOKENS, TOKENS)], sibling)

    x1, x2, y1, by_z, sent_tables, q_copies = {}, {}, {}, {}, [], []
    xs, rows_y = (x, right, across, left), (y_lo, far)

    def forward(piece, k):
        y1[piece, k] = send_y(piece, chip(xs[k]))
        if piece == 0:
            by_z[0, k] = send_z(chip(xs[k]))

    def start_own(piece):
        for copy in own[piece]:
            copy.wait()
        if piece < 3:
            x1[piece, 0] = [send_x(piece, me, core)]
        y1[piece, 0] = [unit(piece, me, core, y_up)]

    def start_other(piece):
        arrive(*sib[piece])
        if piece < 3:
            x1[piece, 0].append(send_x(piece, me, other))
        y1[piece, 0].append(unit(piece, me, other, y_down))

    def start_last():
        x1[3, 0] = [send_x(3, me, core), send_x(3, me, other)]

    def start_far():
        arrive(*y1[3, 0])
        there = chip(x, far)
        x1[3, 1] = [send_x(3, there, core), send_x(3, there, other)]

    def from_left(piece, row):
        arrive(x1[piece, row][0][0], x1[piece, row][1][0])
        x2[piece, row, 0] = unit(piece, chip(left, rows_y[row]), core, x_up)
        if piece < 3:
            forward(piece, 3)

    def from_right(piece, row):
        arrive(x1[piece, row][0][1], x1[piece, row][1][1])
        x2[piece, row, 1] = unit(piece, chip(right, rows_y[row]), other, x_down)
        if piece < 3:
            forward(piece, 1)

    def from_across(piece):
        arrive(x2[piece, 0, 0], x2[piece, 0, 1])
        forward(piece, 2)

    def from_far(k):
        arrive(*y1[0, k])
        by_z[1, k] = send_z(chip(xs[k], far))

    def use(piece, row, k):
        if piece == 0 and (row, k) != (0, 0):
            arrive(*by_z[row, k])
        elif piece in (1, 2) and row == 1:
            arrive(*y1[piece, k])
        elif piece == 3 and k == 2:
            arrive(x2[3, row, 0], x2[3, row, 1])
        if piece == 0 and (row, k) == (0, 0):
            arrive(*sent_tokens)
        add(piece, chip(xs[k], rows_y[row]), (row, k) == (0, 0))

    def make_tables():
        angle = sorted_col * freq[...]
        sign = jnp.where(lax.broadcasted_iota(jnp.int32, (1, HEAD_SIZE), 1) < HEAD_SIZE // 2, -1.0, 1.0)
        tables[0, 0] = jnp.cos(angle)
        tables[0, 1] = jnp.sin(angle) * sign
        sent_tables.append(remote(tables.at[0], tables.at[1], sibling))

    def rotate(value, which):
        return value * tables[which, 0] + pltpu.roll(value, HEAD_SIZE // 2, 1) * tables[which, 1]

    z1, y2, kv_sib, z2, f1, f2 = {}, {}, {}, {}, {}, {}

    def kv_block(head, of_run, part=slice(None)):
        return kv_out.at[head, part, of_run]

    def head_of(piece, whose):
        return (core if whose == 0 else other) * 2 + piece

    def send_kv(piece, whose):
        head = head_of(piece, whose)
        dst = kv_block(head, run)
        src = kv_stage.at[piece, 0] if whose == 0 else dst
        z1[piece, whose] = remote(src, dst, z_up), remote(src, dst, z_down)
        y2[piece, whose] = remote(src, dst, opposite)

    def pass_z(piece, whose, of_y, from_z1):
        head = head_of(piece, whose)
        arrive(*from_z1)
        low, high = pl.ds(0, BLOCKS // 2), pl.ds(BLOCKS // 2, BLOCKS // 2)
        a = kv_block(head, of_y * 4 + z_left, low)
        b = kv_block(head, of_y * 4 + z_right, high)
        return remote(a, a, z_up), remote(b, b, z_down)

    def pass_near(piece, whose):
        z2[piece, whose] = pass_z(piece, whose, y_hi, z1[piece, whose])

    def pass_y(piece, whose):
        arrive(y2[piece, whose])
        ref = kv_block(head_of(piece, whose), (1 - y_hi) * 4 + z)
        f1[piece, whose] = remote(ref, ref, z_up), remote(ref, ref, z_down)

    def pass_far(piece, whose):
        f2[piece, whose] = pass_z(piece, whose, 1 - y_hi, f1[piece, whose])

    pos_z, pos_y, pos_z2 = [], [], []

    def pos_start():
        local(pos_stage, pos_out.at[run])
        pos_z.extend([remote(pos_stage, pos_out.at[run], z_up), remote(pos_stage, pos_out.at[run], z_down)])
        pos_y.append(remote(pos_stage, pos_out.at[run], opposite))

    def pos_near():
        arrive(*pos_z)
        ref = pos_out.at[y_hi * 4 + z_left]
        pos_z2.append(remote(ref, ref, z_up))

    def pos_across():
        arrive(*pos_y)
        ref = pos_out.at[(1 - y_hi) * 4 + z]
        pos_z[:] = [remote(ref, ref, z_up), remote(ref, ref, z_down)]

    def pos_far():
        arrive(*pos_z)
        ref = pos_out.at[(1 - y_hi) * 4 + z_left]
        pos_z2.append(remote(ref, ref, z_up))

    def finish_kv(piece):
        if piece == 0:
            arrive(*sent_tables)
        for s in range(2):
            rows = slice(s * TOKENS, (s + 1) * TOKENS)
            key = rotate(totals[piece][rows, :HEAD_SIZE], s).astype(jnp.bfloat16)
            value = totals[piece][rows, HEAD_SIZE:].astype(jnp.bfloat16)
            kv_stage[piece, s] = jnp.concatenate([key, value], axis=1).reshape(BLOCKS, PART, 2 * HEAD_SIZE)
        dst = kv_block(head_of(piece, 0), run)
        kv_sib[piece] = remote(kv_stage.at[piece, 1], dst, sibling)
        local(kv_stage.at[piece, 0], dst)
        send_kv(piece, 0)

    def second_kv(piece):
        arrive(kv_sib[piece])
        send_kv(piece, 1)

    def finish_q(piece):
        j = piece - 2
        for s in range(2):
            for g in range(4):
                rows = slice(s * TOKENS, (s + 1) * TOKENS)
                cols = slice(g * HEAD_SIZE, (g + 1) * HEAD_SIZE)
                q_stage[j, s, g] = rotate(totals[piece][rows, cols], s).astype(jnp.bfloat16)
        dst = q_out.at[pl.ds((core * 2 + j) * 4, 4)]
        local(q_stage.at[j, 0], dst)
        q_copies.append(remote(q_stage.at[j, 1], dst, sibling))

    sib = [to_sibling(0)]
    start_own(0)
    read.wait()
    sent_tokens = [sort_tokens(0)]
    start_other(0)
    sib.append(to_sibling(1))
    sent_tokens.append(sort_tokens(4))
    sib += [to_sibling(2), to_sibling(3)]

    start_own(3)
    start_own(1)
    from_far(0)
    from_left(0, 0)
    from_right(0, 0)
    pos_start()
    start_other(1)
    make_tables()
    use(0, 0, 0)
    use(1, 0, 0)
    from_across(0)
    start_own(2)
    use(0, 0, 3)
    start_other(3)
    use(0, 1, 0)
    from_left(1, 0)
    pos_near()
    from_far(3)
    from_right(1, 0)
    use(1, 0, 3)
    use(1, 0, 1)
    from_far(1)
    use(3, 0, 0)
    use(1, 1, 0)
    use(0, 0, 2)
    pos_across()
    from_far(2)
    use(0, 1, 3)
    use(0, 0, 1)
    use(0, 1, 1)
    start_last()
    pos_far()
    use(0, 1, 2)
    finish_kv(0)
    from_across(1)
    use(1, 0, 2)
    second_kv(0)
    use(1, 1, 3)
    use(1, 1, 1)
    pass_near(0, 0)
    start_other(2)
    use(2, 0, 0)
    pass_y(0, 0)
    from_left(3, 0)
    from_right(3, 0)
    use(3, 0, 3)
    use(3, 0, 1)
    pass_near(0, 1)
    use(1, 1, 2)
    finish_kv(1)
    second_kv(1)
    from_left(2, 0)
    from_right(2, 0)
    use(2, 0, 1)
    use(2, 0, 3)
    pass_y(0, 1)
    pass_far(0, 0)
    use(2, 1, 0)
    use(3, 0, 2)
    pass_near(1, 0)
    start_far()
    use(3, 1, 0)
    pass_y(1, 0)
    from_across(2)
    use(2, 0, 2)
    pass_near(1, 1)
    pass_y(1, 1)
    pass_far(0, 1)
    use(2, 1, 3)
    from_left(3, 1)
    from_right(3, 1)
    use(3, 1, 3)
    use(3, 1, 1)
    pass_far(1, 0)
    use(2, 1, 1)
    use(2, 1, 2)
    use(3, 1, 2)
    pass_far(1, 1)
    finish_q(3)
    finish_q(2)
    arrive(*pos_z2)
    for key in z2:
        arrive(*z2[key], *f2[key])
    arrive(*q_copies)
    for copy in copies:
        copy.wait_send()
    for copy in locals_[len(locals_) - 5 :]:
        copy.wait()


def projections(tokens, positions, freq, w_query, w_key, w_value):
    anywhere = pl.BlockSpec(memory_space=pl.ANY)
    vmem = pl.BlockSpec(memory_space=pltpu.VMEM)
    wide = 4 * HEAD_SIZE
    return pl.pallas_call(
        projection_kernel,
        out_shape=[
            jax.ShapeDtypeStruct((QUERY_HEADS, TOKENS, HEAD_SIZE), jnp.bfloat16),
            jax.ShapeDtypeStruct((KEY_VALUE_HEADS, BLOCKS, RUNS, PART, 2 * HEAD_SIZE), jnp.bfloat16),
            jax.ShapeDtypeStruct((RUNS, 8, TOKENS), jnp.float32),
        ],
        in_specs=[anywhere, vmem, vmem, anywhere, anywhere, anywhere],
        out_specs=[anywhere] * 3,
        scratch_shapes=[
            pltpu.VMEM((TOKENS, CHIPS * CHUNK), jnp.bfloat16),
            pltpu.VMEM((CHIPS, 2 * TOKENS, CHUNK), jnp.bfloat16),
            pltpu.VMEM((CHIPS, 2, ROWS, 2 * HEAD_SIZE), jnp.bfloat16),
            pltpu.VMEM((CHIPS, 2, ROWS, 2 * HEAD_SIZE), jnp.bfloat16),
            pltpu.VMEM((CHIPS, 2, ROWS, wide), jnp.bfloat16),
            pltpu.VMEM((CHIPS, 2, ROWS, wide), jnp.bfloat16),
            pltpu.VMEM((2 * TOKENS, 2 * HEAD_SIZE), jnp.float32),
            pltpu.VMEM((2 * TOKENS, 2 * HEAD_SIZE), jnp.float32),
            pltpu.VMEM((2 * TOKENS, wide), jnp.float32),
            pltpu.VMEM((2 * TOKENS, wide), jnp.float32),
            pltpu.VMEM((2, 2, TOKENS, HEAD_SIZE), jnp.float32),
            pltpu.VMEM((2, 2, BLOCKS, PART, 2 * HEAD_SIZE), jnp.bfloat16),
            pltpu.VMEM((2, 2, 4, TOKENS, HEAD_SIZE), jnp.bfloat16),
            pltpu.VMEM((8, TOKENS), jnp.float32),
            pltpu.SemaphoreType.DMA((16,)),
            pltpu.SemaphoreType.DMA((COPIES,)),
            pltpu.SemaphoreType.DMA((COPIES,)),
        ],
        compiler_params=pltpu.CompilerParams(
            collective_id=0, has_side_effects=True, vmem_limit_bytes=56 << 20
        ),
        cost_estimate=pl.CostEstimate(flops=10**10, bytes_accessed=2 * 10**7, transcendentals=10**5),
        name="projections",
    )(tokens, positions, freq, w_query, w_key, w_value)


def shards(tokens, positions, segment_ids, w_query, key_weight, value_weight):
    half = HEAD_SIZE // 2
    freq = 500000.0 ** (-jnp.arange(half, dtype=jnp.float32) / half)
    freq = jnp.concatenate([freq, freq])[None, :]
    query, kv, runs = projections(tokens[0], positions, freq, w_query, key_weight, value_weight)
    kv = kv.reshape(KEY_VALUE_HEADS, RUNS * TOKENS, 2 * HEAD_SIZE)
    return attention(query, kv, runs, positions, segment_ids)[None]


def solution(mesh):
    placed = (P("dp", "ctx", None), P("dp", "ctx"), P("dp", None), P("dp", None), P("dp", None), P("dp", None))
    return jax.shard_map(
        shards, mesh=mesh, in_specs=placed, out_specs=P("dp", "ctx", None), check_vma=False
    )
```

```python
import math

import jax
import jax.numpy as jnp
import numpy as np
from jax import lax
from jax.experimental import pallas as pl
from jax.experimental.pallas import tpu as pltpu
from jax.sharding import PartitionSpec as P

QUERY_HEADS = 16
KEY_VALUE_HEADS = 4
HEAD_SIZE = 128
DOCS = 8


RUNS = 8
TOKENS = 384
KEY_BLOCK = 256
QUERY_TILE = 96
GROUP = 4
NEVER = -1e30


def attention_kernel(
    q_hbm, kv_hbm, runs_ref, stored_ref, seg_ref, out_ref,
    q_ref, kv_ref, key_pos, query_at, start_at, top, total, summed, rows_done, sem,
):
    part = KEY_BLOCK // RUNS
    blocks = TOKENS // part
    tiles = TOKENS // QUERY_TILE
    factor = HEAD_SIZE ** -0.5 * math.log2(math.e)
    loads = [pltpu.make_async_copy(q_hbm, q_ref, sem.at[0]), pltpu.make_async_copy(kv_hbm, kv_ref, sem.at[1])]
    for load in loads:
        load.start()

    query_pos = runs_ref[lax.axis_index("ctx")][:1]
    seg = seg_ref[...]
    start = jnp.zeros_like(query_pos)
    for doc in range(1, DOCS):
        before = jnp.sum((seg < doc).astype(jnp.float32), axis=1, keepdims=True)
        start = jnp.where(before <= query_pos, jnp.maximum(start, before), start)

    runs = runs_ref[:, 0]
    for block in range(blocks):
        at = slice(block * part, (block + 1) * part)
        key_pos[block] = jnp.concatenate([runs[run : run + 1, at] for run in range(RUNS)], axis=1)
    query_at[...] = jnp.broadcast_to(jnp.broadcast_to(query_pos, (8, TOKENS)).T[:, :1], (TOKENS, 128))
    start_at[...] = jnp.broadcast_to(jnp.broadcast_to(start, (8, TOKENS)).T[:, :1], (TOKENS, 128))

    lane = lax.broadcasted_iota(jnp.int32, (1, TOKENS), 1) % part
    lowest = jnp.where(lane == 0, jnp.min(runs, axis=0, keepdims=True), 1e9)
    highest = jnp.where(lane == part - 1, jnp.max(runs, axis=0, keepdims=True), 1e9)
    ranges = []
    for tile in range(tiles):
        at = slice(tile * QUERY_TILE, (tile + 1) * QUERY_TILE)
        last = jnp.max(query_pos[:, at], axis=1, keepdims=True)
        first = jnp.min(start[:, at], axis=1, keepdims=True)
        ranges.append((jnp.sum((highest < first).astype(jnp.int32)), jnp.sum((lowest <= last).astype(jnp.int32))))
    for load in loads:
        load.wait()

    for tile in range(tiles):
        at = slice(tile * QUERY_TILE, (tile + 1) * QUERY_TILE)
        begin, end = ranges[tile]
        top[...] = jnp.full_like(top, NEVER)
        total[...] = jnp.zeros_like(total)
        summed[...] = jnp.zeros_like(summed)
        queries = [
            jnp.concatenate([q_ref[head * GROUP + g, at] for g in range(GROUP)], axis=0)
            for head in range(KEY_VALUE_HEADS)
        ]

        def step(block, count):
            rows = pl.ds(pl.multiple_of(block * KEY_BLOCK, KEY_BLOCK), count * KEY_BLOCK)
            pos = jnp.concatenate([key_pos[block + i] for i in range(count)], axis=1)
            lanes = count * KEY_BLOCK // 128
            visible = (pos <= jnp.concatenate([query_at[at]] * lanes, axis=1)) & (
                pos >= jnp.concatenate([start_at[at]] * lanes, axis=1)
            )
            visible = jnp.concatenate([visible] * GROUP, axis=0)
            scores = [
                lax.dot_general(
                    queries[head], kv_ref[head, rows, :HEAD_SIZE], (((1,), (1,)), ((), ())),
                    preferred_element_type=jnp.float32,
                )
                for head in range(KEY_VALUE_HEADS)
            ]
            weights, fades = [], []
            for head in range(KEY_VALUE_HEADS):
                score = jnp.where(visible, scores[head], -jnp.inf)
                old = top[head]
                new = jnp.maximum(old, jnp.max(score, axis=1, keepdims=True))
                weight = jnp.exp2((score - jnp.concatenate([new] * lanes, axis=1)) * factor)
                fade = jnp.exp2((old - new) * factor)
                top[head] = new
                total[head] = total[head] * fade + sum(weight[:, i * 128 : (i + 1) * 128] for i in range(lanes))
                weights.append(weight.astype(jnp.bfloat16))
                fades.append(fade)
            for head in range(KEY_VALUE_HEADS):
                added = jnp.dot(weights[head], kv_ref[head, rows, HEAD_SIZE:], preferred_element_type=jnp.float32)
                summed[head] = summed[head] * fades[head] + added

        fours = (end - begin) // 4
        rest = begin + 4 * fours
        pairs = (end - rest) // 2

        @pl.loop(0, fours)
        def _(four):
            step(begin + 4 * four, 4)

        @pl.loop(0, pairs)
        def _(pair):
            step(rest + 2 * pair, 2)

        @pl.loop(rest + 2 * pairs, end)
        def _(block):
            step(block, 1)

        for head in range(KEY_VALUE_HEADS):
            result = (summed[head] / jnp.sum(total[head], axis=1, keepdims=True)).astype(jnp.bfloat16)
            for g in range(GROUP):
                cols = slice((head * GROUP + g) * HEAD_SIZE, (head * GROUP + g + 1) * HEAD_SIZE)
                rows_done[at, cols] = result[g * QUERY_TILE : (g + 1) * QUERY_TILE]

    stored = jnp.broadcast_to(stored_ref[...].astype(jnp.float32), (8, TOKENS)).T[:, :1]
    turn = (stored == query_pos).astype(jnp.bfloat16)
    wide = 4 * HEAD_SIZE
    for at in range(0, QUERY_HEADS * HEAD_SIZE, wide):
        out_ref[:, at : at + wide] = jnp.dot(
            turn, rows_done[:, at : at + wide], preferred_element_type=jnp.float32
        ).astype(jnp.bfloat16)


def attention(query, kv, runs, stored, seg):
    part = KEY_BLOCK // RUNS
    width = GROUP * QUERY_TILE
    vmem = pl.BlockSpec(memory_space=pltpu.VMEM)
    anywhere = pl.BlockSpec(memory_space=pl.ANY)
    return pl.pallas_call(
        attention_kernel,
        out_shape=jax.ShapeDtypeStruct((TOKENS, QUERY_HEADS * HEAD_SIZE), jnp.bfloat16),
        in_specs=[anywhere, anywhere, vmem, vmem, vmem],
        out_specs=vmem,
        scratch_shapes=[
            pltpu.VMEM((QUERY_HEADS, TOKENS, HEAD_SIZE), jnp.bfloat16),
            pltpu.VMEM((KEY_VALUE_HEADS, RUNS * TOKENS, 2 * HEAD_SIZE), jnp.bfloat16),
            pltpu.VMEM((TOKENS // part, 1, KEY_BLOCK), jnp.float32),
            pltpu.VMEM((TOKENS, 128), jnp.float32),
            pltpu.VMEM((TOKENS, 128), jnp.float32),
            pltpu.VMEM((KEY_VALUE_HEADS, width, 128), jnp.float32),
            pltpu.VMEM((KEY_VALUE_HEADS, width, 128), jnp.float32),
            pltpu.VMEM((KEY_VALUE_HEADS, width, HEAD_SIZE), jnp.float32),
            pltpu.VMEM((TOKENS, QUERY_HEADS * HEAD_SIZE), jnp.bfloat16),
            pltpu.SemaphoreType.DMA((2,)),
        ],
        compiler_params=pltpu.CompilerParams(vmem_limit_bytes=56 << 20),
        cost_estimate=pl.CostEstimate(flops=5 * 10**9, bytes_accessed=11 * 10**6, transcendentals=10**7),
        name="attention",
    )(query, kv, runs, stored, seg)


ROWS = 256
CHIPS = 8
CHUNK = 2 * ROWS
COPIES = 144
PART = KEY_BLOCK // RUNS
BLOCKS = TOKENS // PART


def projection_kernel(
    tokens, positions, freq, w_query, w_key, w_value,
    q_out, kv_out, pos_out,
    stored, tok, weights_a, weights_b, weights_c, weights_d,
    acc_a, acc_b, acc_c, acc_d, tables, kv_stage, q_stage, pos_stage,
    local_sem, send_sem, recv_sem,
):
    dp, ctx = lax.axis_index("dp"), lax.axis_index("ctx")
    core, x, y_lo = dp % 2, (dp // 2) % 4, dp // 8
    y_hi, z = ctx // 4, ctx % 4
    other = 1 - core

    def device(core=core, x=x, y_lo=y_lo, y_hi=y_hi, z=z):
        return ((y_lo * 4 + x) * 2 + core, y_hi * 4 + z)

    right, left, across = (x + 1) % 4, (x + 3) % 4, (x + 2) % 4
    z_right, z_left = (z + 1) % 4, (z + 3) % 4
    far = 1 - y_lo
    y_up = device(y_lo=far, y_hi=(y_hi + y_lo) % 2)
    y_down = device(y_lo=far, y_hi=(y_hi + far) % 2)
    x_up, x_down = device(x=right), device(x=left)
    z_up, z_down = device(z=z_right), device(z=z_left)
    sibling = device(core=other)
    opposite = device(y_hi=1 - y_hi)

    locals_, copies = [], []

    def local(src, dst):
        copy = pltpu.make_async_copy(src, dst, local_sem.at[len(locals_)])
        locals_.append(copy)
        copy.start()
        return copy

    def remote(src, dst, to):
        at = len(copies)
        copy = pltpu.make_async_remote_copy(
            src_ref=src, dst_ref=dst, send_sem=send_sem.at[at], recv_sem=recv_sem.at[at],
            device_id=to, device_id_type=pl.DeviceIdType.MESH,
        )
        copies.append(copy)
        copy.start()
        return copy

    def chip(x, row=y_lo):
        return row * 4 + x

    def columns(ref, start, size):
        return ref.at[:, pl.ds(pl.multiple_of(start, size), size)]

    me = chip(x)
    half = HEAD_SIZE
    buffers = (weights_a, weights_b, weights_c, weights_d)
    totals = (acc_a, acc_b, acc_c, acc_d)

    def sources(piece, of_core):
        if piece < 2:
            start = (of_core * 2 + piece) * half
            return [(columns(w_key, start, half), slice(0, half)), (columns(w_value, start, half), slice(half, 2 * half))]
        start = (of_core * 2 + piece - 2) * 4 * half
        return [(columns(w_query, start, 4 * half), slice(0, 4 * half))]

    own = [[local(src, buffers[p].at[me, core, :, to]) for src, to in sources(p, core)] for p in (0, 1)]
    read = local(tokens, stored)
    own += [[local(src, buffers[p].at[me, core, :, to]) for src, to in sources(p, core)] for p in (2, 3)]

    barrier = pltpu.get_barrier_semaphore()
    partners = (sibling, x_up, x_down, y_up, y_down, z_up, z_down, opposite)
    for partner in partners:
        pl.semaphore_signal(barrier, inc=1, device_id=partner, device_id_type=pl.DeviceIdType.MESH)

    pos_row = positions[...].astype(jnp.float32)
    pos_col = jnp.broadcast_to(pos_row, (8, TOKENS)).T[:, :1]
    rank_row = jnp.sum((pos_col < pos_row).astype(jnp.float32), axis=0, keepdims=True)
    rank_col = jnp.sum((pos_row < pos_col).astype(jnp.float32), axis=1, keepdims=True)
    count_row = lax.broadcasted_iota(jnp.int32, (TOKENS, TOKENS), 1).astype(jnp.float32)
    count_col = lax.broadcasted_iota(jnp.int32, (TOKENS, TOKENS), 0).astype(jnp.float32)
    turn = count_col == rank_row
    sorted_col = jnp.sum(jnp.where(turn, pos_row, 0.0), axis=1, keepdims=True)
    sorted_row = jnp.sum(jnp.where(count_row == rank_col, pos_col, 0.0), axis=0, keepdims=True)
    pos_stage[...] = jnp.broadcast_to(sorted_row, (8, TOKENS))
    turn = turn.astype(jnp.bfloat16)
    run = ctx

    pl.semaphore_wait(barrier, len(partners))

    def to_sibling(piece):
        return [remote(src, buffers[piece].at[me, core, :, to], sibling) for src, to in sources(piece, other)]

    mine = pl.ds(pl.multiple_of((z % 2) * (ROWS // 2), ROWS // 2), ROWS // 2)

    def unit(piece, at, row, to):
        ref = buffers[piece].at[at, row, mine] if piece == 0 else buffers[piece].at[at, row]
        return remote(ref, ref, to)

    def send_z(at):
        return unit(0, at, core, z_up), unit(0, at, other, z_down)

    def send_x(piece, at, row):
        return unit(piece, at, row, x_up), unit(piece, at, row, x_down)

    def send_y(piece, at):
        return unit(piece, at, core, y_up), unit(piece, at, other, y_down)

    def arrive(*some):
        for copy in some:
            copy.wait_recv()

    def add(piece, at, first=False):
        weights = buffers[piece][at]
        product = jnp.dot(
            tok[at], weights.reshape(CHUNK, weights.shape[-1]), preferred_element_type=jnp.float32
        )
        if first:
            totals[piece][...] = product
        else:
            totals[piece][...] += product


    def sort_tokens(first):
        for at in range(first, first + 4):
            tok[at, :TOKENS] = jnp.dot(
                turn, stored[:, at * CHUNK : (at + 1) * CHUNK], preferred_element_type=jnp.float32
            ).astype(jnp.bfloat16)
        some = pl.ds(first, 4)
        return remote(tok.at[some, pl.ds(0, TOKENS)], tok.at[some, pl.ds(TOKENS, TOKENS)], sibling)

    x1, x2, y1, by_z, sent_tables, q_copies = {}, {}, {}, {}, [], []
    xs, rows_y = (x, right, across, left), (y_lo, far)

    def forward(piece, k):
        y1[piece, k] = send_y(piece, chip(xs[k]))
        if piece == 0:
            by_z[0, k] = send_z(chip(xs[k]))

    def start_own(piece):
        for copy in own[piece]:
            copy.wait()
        if piece < 3:
            x1[piece, 0] = [send_x(piece, me, core)]
        y1[piece, 0] = [unit(piece, me, core, y_up)]

    def start_other(piece):
        arrive(*sib[piece])
        if piece < 3:
            x1[piece, 0].append(send_x(piece, me, other))
        y1[piece, 0].append(unit(piece, me, other, y_down))

    def start_last():
        x1[3, 0] = [send_x(3, me, core), send_x(3, me, other)]

    def start_far():
        arrive(*y1[3, 0])
        there = chip(x, far)
        x1[3, 1] = [send_x(3, there, core), send_x(3, there, other)]

    def from_left(piece, row):
        arrive(x1[piece, row][0][0], x1[piece, row][1][0])
        x2[piece, row, 0] = unit(piece, chip(left, rows_y[row]), core, x_up)
        if piece < 3:
            forward(piece, 3)

    def from_right(piece, row):
        arrive(x1[piece, row][0][1], x1[piece, row][1][1])
        x2[piece, row, 1] = unit(piece, chip(right, rows_y[row]), other, x_down)
        if piece < 3:
            forward(piece, 1)

    def from_across(piece):
        arrive(x2[piece, 0, 0], x2[piece, 0, 1])
        forward(piece, 2)

    def from_far(k):
        arrive(*y1[0, k])
        by_z[1, k] = send_z(chip(xs[k], far))

    def use(piece, row, k):
        if piece == 0 and (row, k) != (0, 0):
            arrive(*by_z[row, k])
        elif piece in (1, 2) and row == 1:
            arrive(*y1[piece, k])
        elif piece == 3 and k == 2:
            arrive(x2[3, row, 0], x2[3, row, 1])
        if piece == 0 and (row, k) == (0, 0):
            arrive(*sent_tokens)
        add(piece, chip(xs[k], rows_y[row]), (row, k) == (0, 0))

    def make_tables():
        angle = sorted_col * freq[...]
        sign = jnp.where(lax.broadcasted_iota(jnp.int32, (1, HEAD_SIZE), 1) < HEAD_SIZE // 2, -1.0, 1.0)
        tables[0, 0] = jnp.cos(angle)
        tables[0, 1] = jnp.sin(angle) * sign
        sent_tables.append(remote(tables.at[0], tables.at[1], sibling))

    def rotate(value, which):
        return value * tables[which, 0] + pltpu.roll(value, HEAD_SIZE // 2, 1) * tables[which, 1]

    z1, y2, kv_sib, z2, f1, f2 = {}, {}, {}, {}, {}, {}

    def kv_block(head, of_run, part=slice(None)):
        return kv_out.at[head, part, of_run]

    def head_of(piece, whose):
        return (core if whose == 0 else other) * 2 + piece

    def send_kv(piece, whose):
        head = head_of(piece, whose)
        dst = kv_block(head, run)
        src = kv_stage.at[piece, 0] if whose == 0 else dst
        z1[piece, whose] = remote(src, dst, z_up), remote(src, dst, z_down)
        y2[piece, whose] = remote(src, dst, opposite)

    def pass_z(piece, whose, of_y, from_z1):
        head = head_of(piece, whose)
        arrive(*from_z1)
        low, high = pl.ds(0, BLOCKS // 2), pl.ds(BLOCKS // 2, BLOCKS // 2)
        a = kv_block(head, of_y * 4 + z_left, low)
        b = kv_block(head, of_y * 4 + z_right, high)
        return remote(a, a, z_up), remote(b, b, z_down)

    def pass_near(piece, whose):
        z2[piece, whose] = pass_z(piece, whose, y_hi, z1[piece, whose])

    def pass_y(piece, whose):
        arrive(y2[piece, whose])
        ref = kv_block(head_of(piece, whose), (1 - y_hi) * 4 + z)
        f1[piece, whose] = remote(ref, ref, z_up), remote(ref, ref, z_down)

    def pass_far(piece, whose):
        f2[piece, whose] = pass_z(piece, whose, 1 - y_hi, f1[piece, whose])

    pos_z, pos_y, pos_z2 = [], [], []

    def pos_start():
        local(pos_stage, pos_out.at[run])
        pos_z.extend([remote(pos_stage, pos_out.at[run], z_up), remote(pos_stage, pos_out.at[run], z_down)])
        pos_y.append(remote(pos_stage, pos_out.at[run], opposite))

    def pos_near():
        arrive(*pos_z)
        ref = pos_out.at[y_hi * 4 + z_left]
        pos_z2.append(remote(ref, ref, z_up))

    def pos_across():
        arrive(*pos_y)
        ref = pos_out.at[(1 - y_hi) * 4 + z]
        pos_z[:] = [remote(ref, ref, z_up), remote(ref, ref, z_down)]

    def pos_far():
        arrive(*pos_z)
        ref = pos_out.at[(1 - y_hi) * 4 + z_left]
        pos_z2.append(remote(ref, ref, z_up))

    def finish_kv(piece):
        dst = kv_block(head_of(piece, 0), run)
        for s in range(2):
            if s == 1 and piece == 0:
                arrive(*sent_tables)
            rows = slice(s * TOKENS, (s + 1) * TOKENS)
            key = rotate(totals[piece][rows, :HEAD_SIZE], s).astype(jnp.bfloat16)
            value = totals[piece][rows, HEAD_SIZE:].astype(jnp.bfloat16)
            kv_stage[piece, s] = jnp.concatenate([key, value], axis=1).reshape(BLOCKS, PART, 2 * HEAD_SIZE)
            if s == 0:
                local(kv_stage.at[piece, 0], dst)
                send_kv(piece, 0)
        kv_sib[piece] = remote(kv_stage.at[piece, 1], dst, sibling)

    def second_kv(piece):
        arrive(kv_sib[piece])
        send_kv(piece, 1)

    def finish_q(piece):
        j = piece - 2
        dst = q_out.at[pl.ds((core * 2 + j) * 4, 4)]
        for s in (1, 0):
            for g in range(4):
                rows = slice(s * TOKENS, (s + 1) * TOKENS)
                cols = slice(g * HEAD_SIZE, (g + 1) * HEAD_SIZE)
                q_stage[j, s, g] = rotate(totals[piece][rows, cols], s).astype(jnp.bfloat16)
            if s == 1:
                q_copies.append(remote(q_stage.at[j, 1], dst, sibling))
        local(q_stage.at[j, 0], dst)

    sib = [to_sibling(0)]
    start_own(0)
    read.wait()
    sent_tokens = [sort_tokens(0)]
    start_other(0)
    sib.append(to_sibling(1))
    sent_tokens.append(sort_tokens(4))
    sib += [to_sibling(2), to_sibling(3)]

    start_own(3)
    start_own(1)
    from_far(0)
    from_left(0, 0)
    from_right(0, 0)
    pos_start()
    start_other(1)
    make_tables()
    use(0, 0, 0)
    use(1, 0, 0)
    from_across(0)
    start_own(2)
    use(0, 0, 3)
    start_other(3)
    use(0, 1, 0)
    from_left(1, 0)
    pos_near()
    from_far(3)
    from_right(1, 0)
    use(1, 0, 3)
    use(1, 0, 1)
    from_far(1)
    use(3, 0, 0)
    use(1, 1, 0)
    use(0, 0, 2)
    pos_across()
    from_far(2)
    use(0, 1, 3)
    use(0, 0, 1)
    use(0, 1, 1)
    start_last()
    pos_far()
    use(0, 1, 2)
    finish_kv(0)
    from_across(1)
    use(1, 0, 2)
    second_kv(0)
    use(1, 1, 3)
    use(1, 1, 1)
    pass_near(0, 0)
    start_other(2)
    use(2, 0, 0)
    pass_y(0, 0)
    from_left(3, 0)
    from_right(3, 0)
    use(3, 0, 3)
    use(3, 0, 1)
    pass_near(0, 1)
    use(1, 1, 2)
    finish_kv(1)
    second_kv(1)
    from_left(2, 0)
    from_right(2, 0)
    use(2, 0, 1)
    use(2, 0, 3)
    pass_y(0, 1)
    pass_far(0, 0)
    use(2, 1, 0)
    use(3, 0, 2)
    pass_near(1, 0)
    start_far()
    use(3, 1, 0)
    pass_y(1, 0)
    from_across(2)
    use(2, 0, 2)
    pass_near(1, 1)
    pass_y(1, 1)
    pass_far(0, 1)
    use(2, 1, 3)
    from_left(3, 1)
    from_right(3, 1)
    use(3, 1, 3)
    use(3, 1, 1)
    pass_far(1, 0)
    use(2, 1, 1)
    use(2, 1, 2)
    use(3, 1, 2)
    pass_far(1, 1)
    finish_q(3)
    finish_q(2)
    arrive(*pos_z2)
    for key in z2:
        arrive(*z2[key], *f2[key])
    arrive(*q_copies)
    for copy in copies:
        copy.wait_send()
    for copy in locals_[len(locals_) - 5 :]:
        copy.wait()


def projections(tokens, positions, freq, w_query, w_key, w_value):
    anywhere = pl.BlockSpec(memory_space=pl.ANY)
    vmem = pl.BlockSpec(memory_space=pltpu.VMEM)
    wide = 4 * HEAD_SIZE
    return pl.pallas_call(
        projection_kernel,
        out_shape=[
            jax.ShapeDtypeStruct((QUERY_HEADS, TOKENS, HEAD_SIZE), jnp.bfloat16),
            jax.ShapeDtypeStruct((KEY_VALUE_HEADS, BLOCKS, RUNS, PART, 2 * HEAD_SIZE), jnp.bfloat16),
            jax.ShapeDtypeStruct((RUNS, 8, TOKENS), jnp.float32),
        ],
        in_specs=[anywhere, vmem, vmem, anywhere, anywhere, anywhere],
        out_specs=[anywhere] * 3,
        scratch_shapes=[
            pltpu.VMEM((TOKENS, CHIPS * CHUNK), jnp.bfloat16),
            pltpu.VMEM((CHIPS, 2 * TOKENS, CHUNK), jnp.bfloat16),
            pltpu.VMEM((CHIPS, 2, ROWS, 2 * HEAD_SIZE), jnp.bfloat16),
            pltpu.VMEM((CHIPS, 2, ROWS, 2 * HEAD_SIZE), jnp.bfloat16),
            pltpu.VMEM((CHIPS, 2, ROWS, wide), jnp.bfloat16),
            pltpu.VMEM((CHIPS, 2, ROWS, wide), jnp.bfloat16),
            pltpu.VMEM((2 * TOKENS, 2 * HEAD_SIZE), jnp.float32),
            pltpu.VMEM((2 * TOKENS, 2 * HEAD_SIZE), jnp.float32),
            pltpu.VMEM((2 * TOKENS, wide), jnp.float32),
            pltpu.VMEM((2 * TOKENS, wide), jnp.float32),
            pltpu.VMEM((2, 2, TOKENS, HEAD_SIZE), jnp.float32),
            pltpu.VMEM((2, 2, BLOCKS, PART, 2 * HEAD_SIZE), jnp.bfloat16),
            pltpu.VMEM((2, 2, 4, TOKENS, HEAD_SIZE), jnp.bfloat16),
            pltpu.VMEM((8, TOKENS), jnp.float32),
            pltpu.SemaphoreType.DMA((16,)),
            pltpu.SemaphoreType.DMA((COPIES,)),
            pltpu.SemaphoreType.DMA((COPIES,)),
        ],
        compiler_params=pltpu.CompilerParams(
            collective_id=0, has_side_effects=True, vmem_limit_bytes=56 << 20
        ),
        cost_estimate=pl.CostEstimate(flops=10**10, bytes_accessed=2 * 10**7, transcendentals=10**5),
        name="projections",
    )(tokens, positions, freq, w_query, w_key, w_value)


def shards(tokens, positions, segment_ids, w_query, key_weight, value_weight):
    half = HEAD_SIZE // 2
    freq = 500000.0 ** (-(np.arange(HEAD_SIZE) % half) / half)
    freq = jnp.asarray(freq[None, :], jnp.float32)
    query, kv, runs = projections(tokens[0], positions, freq, w_query, key_weight, value_weight)
    kv = kv.reshape(KEY_VALUE_HEADS, RUNS * TOKENS, 2 * HEAD_SIZE)
    return attention(query, kv, runs, positions, segment_ids)[None]


def solution(mesh):
    placed = (P("dp", "ctx", None), P("dp", "ctx"), P("dp", None), P("dp", None), P("dp", None), P("dp", None))
    return jax.shard_map(
        shards, mesh=mesh, in_specs=placed, out_specs=P("dp", "ctx", None), check_vma=False
    )
```

```python
import math

import jax
import jax.numpy as jnp
import ml_dtypes
import numpy as np
from jax import lax
from jax.experimental import pallas as pl
from jax.experimental.pallas import tpu as pltpu
from jax.sharding import PartitionSpec as P

QUERY_HEADS = 16
KEY_VALUE_HEADS = 4
HEAD_SIZE = 128
DOCS = 8


RUNS = 8
TOKENS = 384
KEY_BLOCK = 256
QUERY_TILE = 96
GROUP = 4
NEVER = -1e30


def attention_kernel(
    q_hbm, kv_hbm, runs_ref, stored_ref, seg_ref, out_hbm,
    q_ref, kv_ref, key_pos, query_at, start_at, top, total, summed, rows_done, out_ref, sem,
):
    part = KEY_BLOCK // RUNS
    blocks = TOKENS // part
    tiles = TOKENS // QUERY_TILE
    factor = HEAD_SIZE ** -0.5 * math.log2(math.e)
    loads = [pltpu.make_async_copy(q_hbm, q_ref, sem.at[0]), pltpu.make_async_copy(kv_hbm, kv_ref, sem.at[1])]
    for load in loads:
        load.start()

    query_pos = runs_ref[lax.axis_index("ctx")][:1]
    seg = seg_ref[...]
    start = jnp.zeros_like(query_pos)
    for doc in range(1, DOCS):
        before = jnp.sum((seg < doc).astype(jnp.float32), axis=1, keepdims=True)
        start = jnp.where(before <= query_pos, jnp.maximum(start, before), start)

    runs = runs_ref[:, 0]
    for block in range(blocks):
        at = slice(block * part, (block + 1) * part)
        key_pos[block] = jnp.concatenate([runs[run : run + 1, at] for run in range(RUNS)], axis=1)
    query_at[...] = jnp.broadcast_to(jnp.broadcast_to(query_pos, (8, TOKENS)).T[:, :1], (TOKENS, 128))
    start_at[...] = jnp.broadcast_to(jnp.broadcast_to(start, (8, TOKENS)).T[:, :1], (TOKENS, 128))

    lane = lax.broadcasted_iota(jnp.int32, (1, TOKENS), 1) % part
    lowest = jnp.where(lane == 0, jnp.min(runs, axis=0, keepdims=True), 1e9)
    highest = jnp.where(lane == part - 1, jnp.max(runs, axis=0, keepdims=True), 1e9)
    ranges = []
    for tile in range(tiles):
        at = slice(tile * QUERY_TILE, (tile + 1) * QUERY_TILE)
        last = jnp.max(query_pos[:, at], axis=1, keepdims=True)
        first = jnp.min(start[:, at], axis=1, keepdims=True)
        ranges.append((jnp.sum((highest < first).astype(jnp.int32)), jnp.sum((lowest <= last).astype(jnp.int32))))
    for load in loads:
        load.wait()

    for tile in range(tiles):
        at = slice(tile * QUERY_TILE, (tile + 1) * QUERY_TILE)
        begin, end = ranges[tile]
        top[...] = jnp.full_like(top, NEVER)
        total[...] = jnp.zeros_like(total)
        summed[...] = jnp.zeros_like(summed)
        queries = [
            jnp.concatenate([q_ref[head * GROUP + g, at] for g in range(GROUP)], axis=0)
            for head in range(KEY_VALUE_HEADS)
        ]

        def step(block, count):
            rows = pl.ds(pl.multiple_of(block * KEY_BLOCK, KEY_BLOCK), count * KEY_BLOCK)
            pos = jnp.concatenate([key_pos[block + i] for i in range(count)], axis=1)
            lanes = count * KEY_BLOCK // 128
            visible = (pos <= jnp.concatenate([query_at[at]] * lanes, axis=1)) & (
                pos >= jnp.concatenate([start_at[at]] * lanes, axis=1)
            )
            visible = jnp.concatenate([visible] * GROUP, axis=0)
            scores = [
                lax.dot_general(
                    queries[head], kv_ref[head, rows, :HEAD_SIZE], (((1,), (1,)), ((), ())),
                    preferred_element_type=jnp.float32,
                )
                for head in range(KEY_VALUE_HEADS)
            ]
            weights, fades = [], []
            for head in range(KEY_VALUE_HEADS):
                score = jnp.where(visible, scores[head], -jnp.inf)
                old = top[head]
                new = jnp.maximum(old, jnp.max(score, axis=1, keepdims=True))
                weight = jnp.exp2((score - jnp.concatenate([new] * lanes, axis=1)) * factor)
                fade = jnp.exp2((old - new) * factor)
                top[head] = new
                total[head] = total[head] * fade + sum(weight[:, i * 128 : (i + 1) * 128] for i in range(lanes))
                weights.append(weight.astype(jnp.bfloat16))
                fades.append(fade)
            for head in range(KEY_VALUE_HEADS):
                added = jnp.dot(weights[head], kv_ref[head, rows, HEAD_SIZE:], preferred_element_type=jnp.float32)
                summed[head] = summed[head] * fades[head] + added

        fours = (end - begin) // 4
        rest = begin + 4 * fours
        pairs = (end - rest) // 2

        @pl.loop(0, fours)
        def _(four):
            step(begin + 4 * four, 4)

        @pl.loop(0, pairs)
        def _(pair):
            step(rest + 2 * pair, 2)

        @pl.loop(rest + 2 * pairs, end)
        def _(block):
            step(block, 1)

        for head in range(KEY_VALUE_HEADS):
            result = (summed[head] / jnp.sum(total[head], axis=1, keepdims=True)).astype(jnp.bfloat16)
            for g in range(GROUP):
                cols = slice((head * GROUP + g) * HEAD_SIZE, (head * GROUP + g + 1) * HEAD_SIZE)
                rows_done[at, cols] = result[g * QUERY_TILE : (g + 1) * QUERY_TILE]

    stored = jnp.broadcast_to(stored_ref[...].astype(jnp.float32), (8, TOKENS)).T[:, :1]
    turn = (stored == query_pos).astype(jnp.bfloat16)
    wide = 4 * HEAD_SIZE
    for at in range(0, QUERY_HEADS * HEAD_SIZE, wide):
        out_ref[:, at : at + wide] = jnp.dot(
            turn, rows_done[:, at : at + wide], preferred_element_type=jnp.float32
        ).astype(jnp.bfloat16)
        leave = pltpu.make_async_copy(out_ref.at[:, at : at + wide], out_hbm.at[:, at : at + wide], sem.at[at // wide])
        leave.start()
        loads.append(leave)
    for leave in loads[2:]:
        leave.wait()


def attention(query, kv, runs, stored, seg):
    part = KEY_BLOCK // RUNS
    width = GROUP * QUERY_TILE
    vmem = pl.BlockSpec(memory_space=pltpu.VMEM)
    anywhere = pl.BlockSpec(memory_space=pl.ANY)
    return pl.pallas_call(
        attention_kernel,
        out_shape=jax.ShapeDtypeStruct((TOKENS, QUERY_HEADS * HEAD_SIZE), jnp.bfloat16),
        in_specs=[anywhere, anywhere, vmem, vmem, vmem],
        out_specs=anywhere,
        scratch_shapes=[
            pltpu.VMEM((QUERY_HEADS, TOKENS, HEAD_SIZE), jnp.bfloat16),
            pltpu.VMEM((KEY_VALUE_HEADS, RUNS * TOKENS, 2 * HEAD_SIZE), jnp.bfloat16),
            pltpu.VMEM((TOKENS // part, 1, KEY_BLOCK), jnp.float32),
            pltpu.VMEM((TOKENS, 128), jnp.float32),
            pltpu.VMEM((TOKENS, 128), jnp.float32),
            pltpu.VMEM((KEY_VALUE_HEADS, width, 128), jnp.float32),
            pltpu.VMEM((KEY_VALUE_HEADS, width, 128), jnp.float32),
            pltpu.VMEM((KEY_VALUE_HEADS, width, HEAD_SIZE), jnp.float32),
            pltpu.VMEM((TOKENS, QUERY_HEADS * HEAD_SIZE), jnp.bfloat16),
            pltpu.VMEM((TOKENS, QUERY_HEADS * HEAD_SIZE), jnp.bfloat16),
            pltpu.SemaphoreType.DMA((4,)),
        ],
        compiler_params=pltpu.CompilerParams(vmem_limit_bytes=56 << 20),
        cost_estimate=pl.CostEstimate(flops=5 * 10**9, bytes_accessed=11 * 10**6, transcendentals=10**7),
        name="attention",
    )(query, kv, runs, stored, seg)


ROWS = 256
CHIPS = 8
CHUNK = 2 * ROWS
COPIES = 144
PART = KEY_BLOCK // RUNS
BLOCKS = TOKENS // PART


def projection_kernel(
    tokens, positions, angles, w_query, w_key, w_value,
    q_out, kv_out, pos_out,
    stored, tok, weights_a, weights_b, weights_c, weights_d,
    acc_a, acc_b, acc_c, acc_d, tables, kv_stage, q_stage, pos_stage,
    local_sem, send_sem, recv_sem,
):
    dp, ctx = lax.axis_index("dp"), lax.axis_index("ctx")
    core, x, y_lo = dp % 2, (dp // 2) % 4, dp // 8
    y_hi, z = ctx // 4, ctx % 4
    other = 1 - core

    def device(core=core, x=x, y_lo=y_lo, y_hi=y_hi, z=z):
        return ((y_lo * 4 + x) * 2 + core, y_hi * 4 + z)

    right, left, across = (x + 1) % 4, (x + 3) % 4, (x + 2) % 4
    z_right, z_left = (z + 1) % 4, (z + 3) % 4
    far = 1 - y_lo
    y_up = device(y_lo=far, y_hi=(y_hi + y_lo) % 2)
    y_down = device(y_lo=far, y_hi=(y_hi + far) % 2)
    x_up, x_down = device(x=right), device(x=left)
    z_up, z_down = device(z=z_right), device(z=z_left)
    sibling = device(core=other)
    opposite = device(y_hi=1 - y_hi)

    locals_, copies = [], []

    def local(src, dst):
        copy = pltpu.make_async_copy(src, dst, local_sem.at[len(locals_)])
        locals_.append(copy)
        copy.start()
        return copy

    def remote(src, dst, to):
        at = len(copies)
        copy = pltpu.make_async_remote_copy(
            src_ref=src, dst_ref=dst, send_sem=send_sem.at[at], recv_sem=recv_sem.at[at],
            device_id=to, device_id_type=pl.DeviceIdType.MESH,
        )
        copies.append(copy)
        copy.start()
        return copy

    def chip(x, row=y_lo):
        return row * 4 + x

    def columns(ref, start, size):
        return ref.at[:, pl.ds(pl.multiple_of(start, size), size)]

    me = chip(x)
    half = HEAD_SIZE
    buffers = (weights_a, weights_b, weights_c, weights_d)
    totals = (acc_a, acc_b, acc_c, acc_d)

    def sources(piece, of_core):
        if piece < 2:
            start = (of_core * 2 + piece) * half
            return [(columns(w_key, start, half), slice(0, half)), (columns(w_value, start, half), slice(half, 2 * half))]
        start = (of_core * 2 + piece - 2) * 4 * half
        return [(columns(w_query, start, 4 * half), slice(0, 4 * half))]

    own = [[local(src, buffers[p].at[me, core, :, to]) for src, to in sources(p, core)] for p in (0, 1)]
    read = local(tokens, stored)
    own += [[local(src, buffers[p].at[me, core, :, to]) for src, to in sources(p, core)] for p in (2, 3)]

    barrier = pltpu.get_barrier_semaphore()
    partners = (sibling, x_up, x_down, y_up, y_down, z_up, z_down, opposite)
    for partner in partners:
        pl.semaphore_signal(barrier, inc=1, device_id=partner, device_id_type=pl.DeviceIdType.MESH)

    pos_row = positions[...].astype(jnp.float32)
    pos_col = jnp.broadcast_to(pos_row, (8, TOKENS)).T[:, :1]
    rank_row = jnp.sum((pos_col < pos_row).astype(jnp.float32), axis=0, keepdims=True)
    rank_col = jnp.sum((pos_row < pos_col).astype(jnp.float32), axis=1, keepdims=True)
    count_row = lax.broadcasted_iota(jnp.int32, (TOKENS, TOKENS), 1).astype(jnp.float32)
    count_col = lax.broadcasted_iota(jnp.int32, (TOKENS, TOKENS), 0).astype(jnp.float32)
    turn = count_col == rank_row
    sorted_col = jnp.sum(jnp.where(turn, pos_row, 0.0), axis=1, keepdims=True)
    sorted_row = jnp.sum(jnp.where(count_row == rank_col, pos_col, 0.0), axis=0, keepdims=True)
    pos_stage[...] = jnp.broadcast_to(sorted_row, (8, TOKENS))
    turn = turn.astype(jnp.bfloat16)
    run = ctx

    pl.semaphore_wait(barrier, len(partners))

    def to_sibling(piece):
        return [remote(src, buffers[piece].at[me, core, :, to], sibling) for src, to in sources(piece, other)]

    mine = pl.ds(pl.multiple_of((z % 2) * (ROWS // 2), ROWS // 2), ROWS // 2)

    def unit(piece, at, row, to):
        ref = buffers[piece].at[at, row, mine] if piece == 0 else buffers[piece].at[at, row]
        return remote(ref, ref, to)

    def send_z(at):
        return unit(0, at, core, z_up), unit(0, at, other, z_down)

    def send_x(piece, at, row):
        return unit(piece, at, row, x_up), unit(piece, at, row, x_down)

    def send_y(piece, at):
        return unit(piece, at, core, y_up), unit(piece, at, other, y_down)

    def arrive(*some):
        for copy in some:
            copy.wait_recv()

    def add(piece, at, first=False):
        weights = buffers[piece][at]
        product = jnp.dot(
            tok[at], weights.reshape(CHUNK, weights.shape[-1]), preferred_element_type=jnp.float32
        )
        if first:
            totals[piece][...] = product
        else:
            totals[piece][...] += product


    def sort_tokens(first):
        for at in range(first, first + 4):
            tok[at, :TOKENS] = jnp.dot(
                turn, stored[:, at * CHUNK : (at + 1) * CHUNK], preferred_element_type=jnp.float32
            ).astype(jnp.bfloat16)
        some = pl.ds(first, 4)
        return remote(tok.at[some, pl.ds(0, TOKENS)], tok.at[some, pl.ds(TOKENS, TOKENS)], sibling)

    x1, x2, y1, by_z, sent_tables, q_copies = {}, {}, {}, {}, [], []
    xs, rows_y = (x, right, across, left), (y_lo, far)

    def forward(piece, k):
        y1[piece, k] = send_y(piece, chip(xs[k]))
        if piece == 0:
            by_z[0, k] = send_z(chip(xs[k]))

    def start_own(piece):
        for copy in own[piece]:
            copy.wait()
        if piece < 3:
            x1[piece, 0] = [send_x(piece, me, core)]
        y1[piece, 0] = [unit(piece, me, core, y_up)]

    def start_other(piece):
        arrive(*sib[piece])
        if piece < 3:
            x1[piece, 0].append(send_x(piece, me, other))
        y1[piece, 0].append(unit(piece, me, other, y_down))

    def start_last():
        x1[3, 0] = [send_x(3, me, core), send_x(3, me, other)]

    def start_far():
        arrive(*y1[3, 0])
        there = chip(x, far)
        x1[3, 1] = [send_x(3, there, core), send_x(3, there, other)]

    def from_left(piece, row):
        arrive(x1[piece, row][0][0], x1[piece, row][1][0])
        x2[piece, row, 0] = unit(piece, chip(left, rows_y[row]), core, x_up)
        if piece < 3:
            forward(piece, 3)

    def from_right(piece, row):
        arrive(x1[piece, row][0][1], x1[piece, row][1][1])
        x2[piece, row, 1] = unit(piece, chip(right, rows_y[row]), other, x_down)
        if piece < 3:
            forward(piece, 1)

    def from_across(piece):
        arrive(x2[piece, 0, 0], x2[piece, 0, 1])
        forward(piece, 2)

    def from_far(k):
        arrive(*y1[0, k])
        by_z[1, k] = send_z(chip(xs[k], far))

    def use(piece, row, k):
        if piece == 0 and (row, k) != (0, 0):
            arrive(*by_z[row, k])
        elif piece in (1, 2) and row == 1:
            arrive(*y1[piece, k])
        elif piece == 3 and k == 2:
            arrive(x2[3, row, 0], x2[3, row, 1])
        if piece == 0 and (row, k) == (0, 0):
            arrive(*sent_tokens)
        add(piece, chip(xs[k], rows_y[row]), (row, k) == (0, 0))

    def make_tables():
        high = jnp.floor(sorted_col * (1.0 / 64))
        lane = lax.broadcasted_iota(jnp.int32, (TOKENS, HEAD_SIZE), 1).astype(jnp.float32)
        pick = ((lane == high) | (lane == sorted_col - 64 * high + 64)).astype(jnp.bfloat16)
        terms = jnp.dot(pick, angles[...], preferred_element_type=jnp.float32)
        size = 4 * HEAD_SIZE
        both = terms[:, :size] + (terms[:, size : 2 * size] + terms[:, 2 * size :])
        cos_a, sin_a, cos_b, sin_b = [both[:, k * HEAD_SIZE : (k + 1) * HEAD_SIZE] for k in range(4)]
        sign = jnp.where(lax.broadcasted_iota(jnp.int32, (1, HEAD_SIZE), 1) < HEAD_SIZE // 2, -1.0, 1.0)
        tables[0, 0] = cos_a * cos_b - sin_a * sin_b
        tables[0, 1] = (sin_a * cos_b + cos_a * sin_b) * sign
        sent_tables.append(remote(tables.at[0], tables.at[1], sibling))

    def rotate(value, which):
        return value * tables[which, 0] + pltpu.roll(value, HEAD_SIZE // 2, 1) * tables[which, 1]

    z1, y2, kv_sib, z2, f1, f2 = {}, {}, {}, {}, {}, {}

    def kv_block(head, of_run, part=slice(None)):
        return kv_out.at[head, part, of_run]

    def head_of(piece, whose):
        return (core if whose == 0 else other) * 2 + piece

    def send_kv(piece, whose):
        head = head_of(piece, whose)
        dst = kv_block(head, run)
        src = kv_stage.at[piece, 0] if whose == 0 else dst
        z1[piece, whose] = remote(src, dst, z_up), remote(src, dst, z_down)
        y2[piece, whose] = remote(src, dst, opposite)

    def pass_z(piece, whose, of_y, from_z1):
        head = head_of(piece, whose)
        arrive(*from_z1)
        low, high = pl.ds(0, BLOCKS // 2), pl.ds(BLOCKS // 2, BLOCKS // 2)
        a = kv_block(head, of_y * 4 + z_left, low)
        b = kv_block(head, of_y * 4 + z_right, high)
        return remote(a, a, z_up), remote(b, b, z_down)

    def pass_near(piece, whose):
        z2[piece, whose] = pass_z(piece, whose, y_hi, z1[piece, whose])

    def pass_y(piece, whose):
        arrive(y2[piece, whose])
        ref = kv_block(head_of(piece, whose), (1 - y_hi) * 4 + z)
        f1[piece, whose] = remote(ref, ref, z_up), remote(ref, ref, z_down)

    def pass_far(piece, whose):
        f2[piece, whose] = pass_z(piece, whose, 1 - y_hi, f1[piece, whose])

    pos_z, pos_y, pos_z2 = [], [], []

    def pos_start():
        local(pos_stage, pos_out.at[run])
        pos_z.extend([remote(pos_stage, pos_out.at[run], z_up), remote(pos_stage, pos_out.at[run], z_down)])
        pos_y.append(remote(pos_stage, pos_out.at[run], opposite))

    def pos_near():
        arrive(*pos_z)
        ref = pos_out.at[y_hi * 4 + z_left]
        pos_z2.append(remote(ref, ref, z_up))

    def pos_across():
        arrive(*pos_y)
        ref = pos_out.at[(1 - y_hi) * 4 + z]
        pos_z[:] = [remote(ref, ref, z_up), remote(ref, ref, z_down)]

    def pos_far():
        arrive(*pos_z)
        ref = pos_out.at[(1 - y_hi) * 4 + z_left]
        pos_z2.append(remote(ref, ref, z_up))

    def finish_kv(piece):
        dst = kv_block(head_of(piece, 0), run)
        for s in range(2):
            if s == 1 and piece == 0:
                arrive(*sent_tables)
            rows = slice(s * TOKENS, (s + 1) * TOKENS)
            key = rotate(totals[piece][rows, :HEAD_SIZE], s).astype(jnp.bfloat16)
            value = totals[piece][rows, HEAD_SIZE:].astype(jnp.bfloat16)
            kv_stage[piece, s] = jnp.concatenate([key, value], axis=1).reshape(BLOCKS, PART, 2 * HEAD_SIZE)
            if s == 0:
                local(kv_stage.at[piece, 0], dst)
                send_kv(piece, 0)
        kv_sib[piece] = remote(kv_stage.at[piece, 1], dst, sibling)

    def second_kv(piece):
        arrive(kv_sib[piece])
        send_kv(piece, 1)

    def finish_q(piece):
        j = piece - 2
        dst = q_out.at[pl.ds((core * 2 + j) * 4, 4)]
        for s in (1, 0):
            for g in range(4):
                rows = slice(s * TOKENS, (s + 1) * TOKENS)
                cols = slice(g * HEAD_SIZE, (g + 1) * HEAD_SIZE)
                q_stage[j, s, g] = rotate(totals[piece][rows, cols], s).astype(jnp.bfloat16)
            if s == 1:
                q_copies.append(remote(q_stage.at[j, 1], dst, sibling))
        local(q_stage.at[j, 0], dst)

    sib = [to_sibling(0)]
    start_own(0)
    read.wait()
    sent_tokens = [sort_tokens(0)]
    start_other(0)
    sib.append(to_sibling(1))
    sent_tokens.append(sort_tokens(4))
    sib += [to_sibling(2), to_sibling(3)]

    start_own(3)
    start_own(1)
    from_far(0)
    from_left(0, 0)
    from_right(0, 0)
    pos_start()
    start_other(1)
    make_tables()
    use(0, 0, 0)
    use(1, 0, 0)
    from_across(0)
    start_own(2)
    use(0, 0, 3)
    start_other(3)
    use(0, 1, 0)
    from_left(1, 0)
    pos_near()
    from_far(3)
    from_right(1, 0)
    use(1, 0, 3)
    use(1, 0, 1)
    from_far(1)
    use(3, 0, 0)
    use(1, 1, 0)
    use(0, 0, 2)
    pos_across()
    from_far(2)
    use(0, 1, 3)
    use(0, 0, 1)
    use(0, 1, 1)
    start_last()
    pos_far()
    use(0, 1, 2)
    finish_kv(0)
    from_across(1)
    use(1, 0, 2)
    second_kv(0)
    use(1, 1, 3)
    use(1, 1, 1)
    pass_near(0, 0)
    start_other(2)
    use(2, 0, 0)
    pass_y(0, 0)
    from_left(3, 0)
    from_right(3, 0)
    use(3, 0, 3)
    use(3, 0, 1)
    pass_near(0, 1)
    use(1, 1, 2)
    finish_kv(1)
    second_kv(1)
    from_left(2, 0)
    from_right(2, 0)
    use(2, 0, 1)
    use(2, 0, 3)
    pass_y(0, 1)
    pass_far(0, 0)
    use(2, 1, 0)
    use(3, 0, 2)
    pass_near(1, 0)
    start_far()
    use(3, 1, 0)
    pass_y(1, 0)
    from_across(2)
    use(2, 0, 2)
    pass_near(1, 1)
    pass_y(1, 1)
    pass_far(0, 1)
    use(2, 1, 3)
    from_left(3, 1)
    from_right(3, 1)
    use(3, 1, 3)
    use(3, 1, 1)
    pass_far(1, 0)
    use(2, 1, 1)
    use(2, 1, 2)
    use(3, 1, 2)
    pass_far(1, 1)
    finish_q(3)
    finish_q(2)
    arrive(*pos_z2)
    for key in z2:
        arrive(*z2[key], *f2[key])
    arrive(*q_copies)
    for copy in copies:
        copy.wait_send()
    for copy in locals_[len(locals_) - 5 :]:
        copy.wait()


def angle_terms():
    half = HEAD_SIZE // 2
    freq = 500000.0 ** (-(np.arange(HEAD_SIZE) % half) / half)
    table = np.zeros((128, 4, HEAD_SIZE))
    coarse = 64 * np.arange(48)[:, None] * freq
    fine = np.arange(64)[:, None] * freq
    table[:48, 0], table[:48, 1] = np.cos(coarse), np.sin(coarse)
    table[64:, 2], table[64:, 3] = np.cos(fine), np.sin(fine)
    rest, terms = table.reshape(128, 4 * HEAD_SIZE), []
    for _ in range(3):
        terms.append(rest.astype(ml_dtypes.bfloat16))
        rest = rest - terms[-1].astype(np.float64)
    return jnp.asarray(np.concatenate(terms, axis=1))


def projections(tokens, positions, angles, w_query, w_key, w_value):
    anywhere = pl.BlockSpec(memory_space=pl.ANY)
    vmem = pl.BlockSpec(memory_space=pltpu.VMEM)
    wide = 4 * HEAD_SIZE
    return pl.pallas_call(
        projection_kernel,
        out_shape=[
            jax.ShapeDtypeStruct((QUERY_HEADS, TOKENS, HEAD_SIZE), jnp.bfloat16),
            jax.ShapeDtypeStruct((KEY_VALUE_HEADS, BLOCKS, RUNS, PART, 2 * HEAD_SIZE), jnp.bfloat16),
            jax.ShapeDtypeStruct((RUNS, 8, TOKENS), jnp.float32),
        ],
        in_specs=[anywhere, vmem, vmem, anywhere, anywhere, anywhere],
        out_specs=[anywhere] * 3,
        scratch_shapes=[
            pltpu.VMEM((TOKENS, CHIPS * CHUNK), jnp.bfloat16),
            pltpu.VMEM((CHIPS, 2 * TOKENS, CHUNK), jnp.bfloat16),
            pltpu.VMEM((CHIPS, 2, ROWS, 2 * HEAD_SIZE), jnp.bfloat16),
            pltpu.VMEM((CHIPS, 2, ROWS, 2 * HEAD_SIZE), jnp.bfloat16),
            pltpu.VMEM((CHIPS, 2, ROWS, wide), jnp.bfloat16),
            pltpu.VMEM((CHIPS, 2, ROWS, wide), jnp.bfloat16),
            pltpu.VMEM((2 * TOKENS, 2 * HEAD_SIZE), jnp.float32),
            pltpu.VMEM((2 * TOKENS, 2 * HEAD_SIZE), jnp.float32),
            pltpu.VMEM((2 * TOKENS, wide), jnp.float32),
            pltpu.VMEM((2 * TOKENS, wide), jnp.float32),
            pltpu.VMEM((2, 2, TOKENS, HEAD_SIZE), jnp.float32),
            pltpu.VMEM((2, 2, BLOCKS, PART, 2 * HEAD_SIZE), jnp.bfloat16),
            pltpu.VMEM((2, 2, 4, TOKENS, HEAD_SIZE), jnp.bfloat16),
            pltpu.VMEM((8, TOKENS), jnp.float32),
            pltpu.SemaphoreType.DMA((16,)),
            pltpu.SemaphoreType.DMA((COPIES,)),
            pltpu.SemaphoreType.DMA((COPIES,)),
        ],
        compiler_params=pltpu.CompilerParams(
            collective_id=0, has_side_effects=True, vmem_limit_bytes=56 << 20
        ),
        cost_estimate=pl.CostEstimate(flops=10**10, bytes_accessed=2 * 10**7, transcendentals=10**5),
        name="projections",
    )(tokens, positions, angles, w_query, w_key, w_value)


def shards(tokens, positions, segment_ids, w_query, key_weight, value_weight):
    query, kv, runs = projections(tokens[0], positions, angle_terms(), w_query, key_weight, value_weight)
    kv = kv.reshape(KEY_VALUE_HEADS, RUNS * TOKENS, 2 * HEAD_SIZE)
    return attention(query, kv, runs, positions, segment_ids)[None]


def solution(mesh):
    placed = (P("dp", "ctx", None), P("dp", "ctx"), P("dp", None), P("dp", None), P("dp", None), P("dp", None))
    return jax.shard_map(
        shards, mesh=mesh, in_specs=placed, out_specs=P("dp", "ctx", None), check_vma=False
    )
```
